128 devices in a mesh: wide: 32 (over y, z, core), narrow: 4 (over x).
Axes of the slice: x: 4, y: 4, z: 4, core: 2. Of those that a mesh axis runs over, the one named last changes fastest.
Arguments:
- superheat_excess: float32 [128, 512, 512], P('wide', 'narrow'), may hold values from -6 to 6
- liquid_indicator: int32 [128, 512, 512], P('wide', 'narrow'), may hold values from 0 to 1, as said below
- group_patch_listing_table: int32 [32, 4, 16], P('wide', 'narrow'), may hold values from -1 to 31, as said below
- source_smearing_factors_north: float32 [16, 16], replicated, may hold values from 0 to 2, as said below
- source_smearing_factors_east: float32 [128, 128], replicated, may hold values from 0 to 2, as said below
Outputs:
- temperature_next: float32 [128, 512, 512], P('wide', 'narrow')
- pressure: float32 [128, 512, 512], P('wide', 'narrow')
- residual: float32 [128, 512, 512], P('wide', 'narrow')
The draws below stay inside these ranges and needn't reach their ends.
Inputs may be any that keep to these rules, and one draw needn't show every extreme that they name: In each row group_patch_listing_table[w, n] the listed tile numbers come first and are distinct, the remaining entries are -1. A row lists 1 to 16 tiles; for every w the rows n < 4 list exactly 32 tiles together, and one of them lists 16. `liquid_indicator`: phase is 1 in every cell outside the listed tiles. `source_smearing_factors_north`: the identity plus entries drawn in 0 to 1.2 / 16. `source_smearing_factors_east`: the identity plus entries drawn in 0 to 1.2 / 128.
All inputs are finite; a program needn't handle non-finite values.
Results may differ from the reference program's by a relative error of at most 0.0003.
Values sent between devices are 32-bit elements; how exact they have to be, the bound alone decides.
A program may use at most 64 MiB of HBM per device.

```python
import math
import jax
import jax.numpy as jnp
from jax import lax

MESH_SPAN_EAST = 512
MESH_SPAN_NORTH = 512
CZ = 4
TY = 16
TX = 128
ITERS = 3
MESH_SPAN_UPWARD = 128
NYD = 128
TPD = 32
MAXT = 16
N_WIDE = 32
N_NARROW = 4


def tile_layout(key):
    base = jax.random.fold_in(key, 4242)
    heavy_key, split_key, order_key, coin_key = jax.random.split(base, 4)
    heaviest = jax.random.randint(heavy_key, (N_WIDE,), 0, N_NARROW)

    def light_counts(subkey):
        picks = jax.random.permutation(subkey, MAXT - 1)[:N_NARROW - 2].astype(jnp.int32) + 1
        edges = jnp.concatenate([jnp.zeros((1,), jnp.int32), jnp.sort(picks), jnp.full((1,), MAXT, jnp.int32)])
        return edges[1:] - edges[:-1]
    lighter = jax.vmap(light_counts)(jax.random.split(split_key, N_WIDE))
    lanes = jnp.arange(N_NARROW, dtype=jnp.int32)[None, :]
    others = jnp.clip(lanes - (lanes > heaviest[:, None]).astype(jnp.int32), 0, N_NARROW - 2)
    counts = jnp.where(lanes == heaviest[:, None], MAXT, jnp.take_along_axis(lighter, others, axis=1))
    orders = jax.vmap(lambda subkey: jax.random.permutation(subkey, TPD))(jax.random.split(order_key, N_WIDE * N_NARROW))
    orders = orders.reshape(N_WIDE, N_NARROW, TPD)[:, :, :MAXT].astype(jnp.int32)
    places = jnp.arange(MAXT, dtype=jnp.int32)
    listing = jnp.where(places[None, None, :] < counts[:, :, None], orders, -1).astype(jnp.int32)
    flags = jnp.any(listing[:, :, :, None] == jnp.arange(TPD, dtype=jnp.int32)[None, None, None, :], axis=2)
    return (listing, flags, coin_key)


def draw_liquid_indicator(key, part):
    listing, flags, coin_key = tile_layout(key)
    coins = jax.random.randint(coin_key, (MESH_SPAN_UPWARD, MESH_SPAN_NORTH, MESH_SPAN_EAST), 0, 2)
    tiles_y = NYD // TY
    tiles_x = MESH_SPAN_EAST // TX
    marked = flags.reshape(N_WIDE, 1, N_NARROW, tiles_y, 1, tiles_x, 1)
    marked = jnp.broadcast_to(marked, (N_WIDE, CZ, N_NARROW, tiles_y, TY, tiles_x, TX)).reshape(MESH_SPAN_UPWARD, MESH_SPAN_NORTH, MESH_SPAN_EAST)
    return jnp.where(marked, coins, 1).astype(jnp.int32)


def draw_group_patch_listing_table(key, part):
    return tile_layout(key)[0]


def draw_source_smearing_factors_north(key, part):
    spread = jax.random.uniform(jax.random.fold_in(key, 31), (TY, TY), jnp.float32, 0.0, 1.2 / TY)
    return jnp.eye(TY, dtype=jnp.float32) + spread


def draw_source_smearing_factors_east(key, part):
    spread = jax.random.uniform(jax.random.fold_in(key, 37), (TX, TX), jnp.float32, 0.0, 1.2 / TX)
    return jnp.eye(TX, dtype=jnp.float32) + spread


def level_of(key, shape, cuts, smallest, largest):
    def one(position, parts):
        steps = jax.random.uniform(jax.random.fold_in(jax.random.fold_in(key, 6), position), (parts,), jnp.float32, smallest / len(cuts), largest / len(cuts))
        return jnp.repeat(jnp.exp(steps), shape[position] // parts).reshape((-1,) + (1,) * (len(shape) - position - 1))

    gain = one(*cuts[0])
    for cut in cuts[1:]:
        gain = gain * one(*cut)
    return gain


def gaussian(key, shape, width, reach, cuts=(), kind=jnp.bfloat16):
    entries = jax.random.normal(key, shape, jnp.float32) * width
    if len(cuts) > 0:
        entries = level_of(key, shape, cuts, -0.22, 0.18) * entries
    return jnp.clip(entries, min=-reach, max=reach).astype(kind)


def setup_inputs(seed: int = 0) -> dict:
    streams_of = jax.random.split(jax.random.key(seed), 6)
    superheat_excess = gaussian(streams_of[0], (MESH_SPAN_UPWARD, MESH_SPAN_NORTH, MESH_SPAN_EAST), 1.0, 6.0, ((0, 32), (1, 4)), jnp.float32)
    liquid_indicator = draw_liquid_indicator(jax.random.fold_in(streams_of[5], 71), 0)
    group_patch_listing_table = draw_group_patch_listing_table(jax.random.fold_in(streams_of[5], 71), 0)
    source_smearing_factors_north = draw_source_smearing_factors_north(jax.random.fold_in(streams_of[5], 71), 0)
    source_smearing_factors_east = draw_source_smearing_factors_east(jax.random.fold_in(streams_of[5], 71), 0)
    return {"superheat_excess": superheat_excess, "liquid_indicator": liquid_indicator, "group_patch_listing_table": group_patch_listing_table, "source_smearing_factors_north": source_smearing_factors_north, "source_smearing_factors_east": source_smearing_factors_east}


conduct_liquid = 1.0
conduct_vapor = 0.4
diffusion = 0.06
mobility_liquid = 1.0
mobility_vapor = 4.0
expansion = 0.3
compress = 0.01
highest = lax.Precision.HIGHEST

def centre(padded):
    return padded[1:-1, 1:-1, 1:-1]

def neighbours(padded):
    return [padded[2:, 1:-1, 1:-1], padded[:-2, 1:-1, 1:-1], padded[1:-1, 2:, 1:-1], padded[1:-1, :-2, 1:-1], padded[1:-1, 1:-1, 2:], padded[1:-1, 1:-1, :-2]]

def heat_advance(temp_pad, liquid_indicator_haloed, inner_region_haloed):
    current = centre(temp_pad)
    phases = centre(liquid_indicator_haloed)
    conduct = jnp.where(phases > 0.5, conduct_liquid, conduct_vapor)
    flux = jnp.zeros_like(current)
    faces = jnp.zeros_like(current)
    for near_temp, near_phase, near_inside in zip(neighbours(temp_pad), neighbours(liquid_indicator_haloed), neighbours(inner_region_haloed)):
        differ = jnp.abs(near_phase - phases) > 0.5
        flux = flux + near_inside * jnp.where(differ, -2.0 * current, near_temp - current)
        faces = faces + near_inside * jnp.where(differ, 1.0, 0.0)
    heated_values = current + diffusion * conduct * flux
    vaporised_amount = 2.0 * conduct * faces * heated_values
    return (heated_values, vaporised_amount)

def face_weights(liquid_indicator_haloed, inner_region_haloed):
    mobility = jnp.where(liquid_indicator_haloed > 0.5, mobility_liquid, mobility_vapor)
    own = centre(mobility)
    return [near_inside * 0.5 * (own + near_mob) for near_inside, near_mob in zip(neighbours(inner_region_haloed), neighbours(mobility))]

def apply_operator(field_pad, weights):
    field = centre(field_pad)
    total = compress * field
    for weight, near in zip(weights, neighbours(field_pad)):
        total = total + weight * (field - near)
    return total

def smear_tiles(tiles, source_smearing_factors_north, source_smearing_factors_east):
    across = jnp.einsum('...bc,dc->...bd', tiles, source_smearing_factors_east, precision=highest)
    return expansion * jnp.einsum('ab,...bd->...ad', source_smearing_factors_north, across, precision=highest)

def cosine_rows(extent, kfirst, klength, cfirst, clength):
    waves = kfirst + jnp.arange(klength, dtype=jnp.int32)
    centres = 2 * (cfirst + jnp.arange(clength, dtype=jnp.int32)) + 1
    turns = waves[:, None] * centres[None, :] % (4 * extent)
    angles = 2.0 * math.pi / (4 * extent) * turns.astype(jnp.float32)
    scales = jnp.where(waves == 0, math.sqrt(1.0 / extent), math.sqrt(2.0 / extent)).astype(jnp.float32)
    return scales[:, None] * jnp.cos(angles)

def eigen(extent, first, length):
    waves = (first + jnp.arange(length, dtype=jnp.int32)).astype(jnp.float32)
    return 4.0 * jnp.sin(waves * (math.pi / (2 * extent))) ** 2

def tile_source(vaporised_amount, group_patch_listing_table, source_smearing_factors_north, source_smearing_factors_east):
    size_y = source_smearing_factors_north.shape[0]
    size_x = source_smearing_factors_east.shape[0]
    tiles_y = MESH_SPAN_NORTH // N_NARROW // size_y
    tiles_x = MESH_SPAN_EAST // size_x
    blocks = vaporised_amount.reshape(N_WIDE, CZ, N_NARROW, tiles_y, size_y, tiles_x, size_x)
    blocks = blocks.transpose(0, 2, 3, 5, 1, 4, 6).reshape(N_WIDE, N_NARROW, tiles_y * tiles_x, CZ, size_y, size_x)
    numbers = jnp.arange(tiles_y * tiles_x, dtype=jnp.int32)
    listed = jnp.any(group_patch_listing_table[:, :, :, None] == numbers[None, None, None, :], axis=2)
    smeared = smear_tiles(blocks, source_smearing_factors_north, source_smearing_factors_east) * listed[:, :, :, None, None, None].astype(jnp.float32)
    smeared = smeared.reshape(N_WIDE, N_NARROW, tiles_y, tiles_x, CZ, size_y, size_x)
    return smeared.transpose(0, 4, 1, 2, 5, 3, 6).reshape(MESH_SPAN_UPWARD, MESH_SPAN_NORTH, MESH_SPAN_EAST)

def precondition(remainder):
    table_x = cosine_rows(MESH_SPAN_EAST, 0, MESH_SPAN_EAST, 0, MESH_SPAN_EAST)
    table_y = cosine_rows(MESH_SPAN_NORTH, 0, MESH_SPAN_NORTH, 0, MESH_SPAN_NORTH)
    table_z = cosine_rows(MESH_SPAN_UPWARD, 0, MESH_SPAN_UPWARD, 0, MESH_SPAN_UPWARD)
    spectrum = jnp.einsum('zyx,kx->zyk', remainder, table_x, precision=highest)
    spectrum = jnp.einsum('zyk,ly->zlk', spectrum, table_y, precision=highest)
    spectrum = jnp.einsum('zlk,mz->mlk', spectrum, table_z, precision=highest)
    denom = eigen(MESH_SPAN_UPWARD, 0, MESH_SPAN_UPWARD)[:, None, None] + eigen(MESH_SPAN_NORTH, 0, MESH_SPAN_NORTH)[None, :, None] + eigen(MESH_SPAN_EAST, 0, MESH_SPAN_EAST)[None, None, :] + compress
    spectrum = spectrum / denom
    spectrum = jnp.einsum('mlk,mz->zlk', spectrum, table_z, precision=highest)
    spectrum = jnp.einsum('zlk,ly->zyk', spectrum, table_y, precision=highest)
    return jnp.einsum('zyk,kx->zyx', spectrum, table_x, precision=highest)

def reference(superheat_excess, liquid_indicator, group_patch_listing_table, source_smearing_factors_north, source_smearing_factors_east):
    liquid_indicator_haloed = jnp.pad(liquid_indicator.astype(jnp.float32), 1)
    inner_region_haloed = jnp.pad(jnp.ones(liquid_indicator.shape, jnp.float32), 1)
    heated_values, vaporised_amount = heat_advance(jnp.pad(superheat_excess, 1), liquid_indicator_haloed, inner_region_haloed)
    source = tile_source(vaporised_amount, group_patch_listing_table, source_smearing_factors_north, source_smearing_factors_east)
    weights = face_weights(liquid_indicator_haloed, inner_region_haloed)
    pressure = jnp.zeros_like(source)
    residual = source
    search = precondition(residual)
    aligned = jnp.sum(residual * search)
    direction = search
    for iteration in range(ITERS):
        image = apply_operator(jnp.pad(direction, 1), weights)
        alpha = aligned / jnp.sum(direction * image)
        pressure = pressure + alpha * direction
        residual = residual - alpha * image
        if iteration + 1 < ITERS:
            search = precondition(residual)
            renewed = jnp.sum(residual * search)
            direction = search + renewed / aligned * direction
            aligned = renewed
    return (heated_values, pressure, residual)
```

```python
import functools
import math

import jax
import jax.numpy as jnp
import ml_dtypes
import numpy as np
from jax import lax
from jax.experimental import pallas as pl
from jax.experimental.pallas import tpu as pltpu
from jax.sharding import PartitionSpec as P

MESH = pl.DeviceIdType.MESH
F32 = jnp.float32
BF16 = jnp.bfloat16
NX, NY, NZ = 512, 512, 128
NW, NN = 32, 4
ND = NW * NN
ITERS = 3
ROWS = 512
FWD, INV = 3, 3


def cosine_np(m):
    k = np.arange(m)[:, None]
    i = np.arange(m)[None, :]
    scale = np.where(k == 0, math.sqrt(1.0 / m), math.sqrt(2.0 / m))
    return scale * np.cos(np.pi * ((k * (2 * i + 1)) % (4 * m)) / (2 * m))


def eigen_np(m):
    return 4.0 * np.sin(np.pi * np.arange(m) / (2 * m)) ** 2


def split_np(table):
    parts = []
    rest = table.astype(np.float64)
    for _ in range(3):
        part = rest.astype(np.float32).astype(ml_dtypes.bfloat16)
        parts.append(part)
        rest = rest - part.astype(np.float64)
    return np.stack(parts)


def z_table():
    table = cosine_np(NZ).reshape(NZ, NW, 2, 2).transpose(0, 3, 1, 2)
    big = np.zeros((NZ, 4, 2, NW, 2, 4))
    for k in range(4):
        big[:, k, :, :, :, k] = table
    return big.reshape(ROWS, ROWS)


def split(x, parts):
    out = []
    for i in range(parts):
        part = x.astype(BF16)
        out.append(part)
        if i + 1 < parts:
            x = x - part.astype(F32)
    return out


PAIRS = {3: ((0, 1), (1, 0), (0, 0)), 6: ((1, 1), (0, 2), (2, 0), (0, 1), (1, 0), (0, 0))}


def product(a, b, dims, passes):
    total = None
    for i, j in PAIRS[passes]:
        term = lax.dot_general(a[i], b[j], (dims, ((), ())), preferred_element_type=F32)
        total = term if total is None else total + term
    return total


def peer(step, w, n):
    dx, dy, dz, dc = step % 4, (step // 4) % 4, (step // 16) % 4, step // 64
    y, z, c = w // 8, (w // 2) % 4, w % 2
    return ((y + dy) % 4) * 8 + ((z + dz) % 4) * 2 + (c + dc) % 2, (n + dx) % 4


def whole_kernel(
    temp_ref, phase_ref, table_ref, north_ref, east_ref, tx_ref, ty_ref, b_ref, bt_ref, rowden_ref, colden_ref,
    tnext_ref, press_ref, resid_ref,
    tpad, ppad, spad, wts, mass, f_ref, c_ref, d_ref, inv_ref,
    sbf, sbi, recvf, recvi, ag_a, ag_b,
    sem_fs, sem_fr, sem_is, sem_ir, sem_as, sem_ar, sem_bs, sem_br, sem_hs, sem_hr,
):
    w = lax.axis_index("wide")
    n = lax.axis_index("narrow")
    me = n * NW + w

    barrier = pltpu.get_barrier_semaphore()

    def greet(step, carry):
        pw, pn = peer(step, w, n)
        pl.semaphore_signal(barrier, inc=1, device_id=(pw, pn), device_id_type=MESH)
        return carry

    lax.fori_loop(1, ND, greet, 0)

    tpad[1:5, 8:136, :] = temp_ref[...]
    ppad[1:5, 8:136, :] = phase_ref[...]
    inv_ref[...] = 1.0 / (rowden_ref[...] + colden_ref[...])
    c_ref[...] = jnp.zeros_like(c_ref)
    d_ref[...] = jnp.zeros_like(d_ref)
    press_ref[...] = jnp.zeros_like(press_ref)
    ag_a[0, me] = jnp.ones((1, 128), F32)

    pl.semaphore_wait(barrier, ND - 1)

    w_up, w_down = (w + 1) % NW, (w + NW - 1) % NW
    n_up, n_down = (n + 1) % NN, (n + NN - 1) % NN

    def halo(slot, src, at, dst):
        moves = (
            (src(3, pl.ds(at, 128)), dst(0, pl.ds(8, 128)), (w_up, n)),
            (src(0, pl.ds(at, 128)), dst(5, pl.ds(8, 128)), (w_down, n)),
            (src(pl.ds(0, 4), pl.ds(at + 120, 8)), dst(pl.ds(1, 4), pl.ds(0, 8)), (w, n_up)),
            (src(pl.ds(0, 4), pl.ds(at, 8)), dst(pl.ds(1, 4), pl.ds(136, 8)), (w, n_down)),
        )
        copies = []
        for i, (a, b, to) in enumerate(moves):
            copies.append(
                pltpu.make_async_remote_copy(
                    src_ref=a,
                    dst_ref=b,
                    send_sem=sem_hs.at[slot, i],
                    recv_sem=sem_hr.at[slot, i],
                    device_id=to,
                    device_id_type=MESH,
                )
            )
        return copies

    head = halo(0, lambda z, y: temp_ref.at[z, y], 0, lambda z, y: tpad.at[z, y])
    head += halo(1, lambda z, y: phase_ref.at[z, y], 0, lambda z, y: ppad.at[z, y])
    for copy in head:
        copy.start()
    for copy in head:
        copy.wait()

    row8 = lax.broadcasted_iota(jnp.int32, (8, NX), 0)
    lane8 = lax.broadcasted_iota(jnp.int32, (8, NX), 1)

    def around(pad, z, i):
        mid = pl.ds(pl.multiple_of(8 + 8 * i, 8), 8)
        low = pl.ds(pl.multiple_of(8 * i, 8), 8)
        high = pl.ds(pl.multiple_of(16 + 8 * i, 8), 8)
        c = pad[z + 1, mid, :]
        up = pad[z + 1, high, :]
        down = pad[z + 1, low, :]
        near = (
            pad[z + 2, mid, :],
            pad[z, mid, :],
            pltpu.roll(jnp.where(row8 == 0, up, c), 7, 0),
            pltpu.roll(jnp.where(row8 == 7, down, c), 1, 0),
            pltpu.roll(c, NX - 1, 1),
            pltpu.roll(c, 1, 1),
        )
        return c, near

    def head_chunk(g, carry):
        z, i = g // 16, g % 16
        rows = pl.ds(pl.multiple_of(8 * g, 8), 8)
        c, near = around(tpad, z, i)
        pc, pnear = around(ppad, z, i)
        gz = jnp.zeros_like(row8) + (4 * w + z)
        gy = row8 + (n * 128 + 8 * i)
        inside = (gz < NZ - 1, gz > 0, gy < NY - 1, gy > 0, lane8 < NX - 1, lane8 > 0)
        conduct = jnp.where(pc > 0, 1.0, 0.4)
        beta = jnp.where(pc > 0, 1.0, 4.0)
        flux = jnp.zeros_like(c)
        faces = jnp.zeros_like(c)
        for q in range(6):
            ins = jnp.where(inside[q], 1.0, 0.0)
            differ = pnear[q] != pc
            flux = flux + ins * jnp.where(differ, -2.0 * c, near[q] - c)
            faces = faces + ins * jnp.where(differ, 1.0, 0.0)
            wts[q, rows, :] = ins * (0.5 * (beta + jnp.where(pnear[q] > 0, 1.0, 4.0)) - 1.0)
        heated = c + 0.06 * conduct * flux
        tnext_ref[z, pl.ds(pl.multiple_of(8 * i, 8), 8), :] = heated
        mass[rows, :] = 2.0 * conduct * faces * heated
        return carry

    lax.fori_loop(0, 64, head_chunk, 0)

    ra = lax.broadcasted_iota(jnp.int32, (128, 16), 0)
    ca = lax.broadcasted_iota(jnp.int32, (128, 16), 1)
    pick = jnp.where(ra % 16 == ca, 1.0, 0.0).astype(F32)
    rb = lax.broadcasted_iota(jnp.int32, (128, 128), 0)
    cb = lax.broadcasted_iota(jnp.int32, (128, 128), 1)
    hp = lax.Precision.HIGHEST
    spread = lax.dot_general(pick, north_ref[...], (((1,), (0,)), ((), ())), precision=hp, preferred_element_type=F32)
    spread = lax.dot_general(spread, pick, (((1,), (1,)), ((), ())), precision=hp, preferred_element_type=F32)
    north_all = jnp.where(rb // 16 == cb // 16, spread, 0.0)
    east = east_ref[...]
    for t in range(4):
        lanes = slice(t * 128, (t + 1) * 128)
        across = lax.dot_general(mass[:, lanes], east, (((1,), (1,)), ((), ())), precision=hp, preferred_element_type=F32)
        tile = (rb // 16) * 4 + t
        listed = jnp.zeros((128, 128), F32)
        for e in range(16):
            listed = jnp.where(tile == table_ref[e], 0.3, listed)
        for z in range(4):
            src = lax.dot_general(
                north_all, across[z * 128 : (z + 1) * 128], (((1,), (0,)), ((), ())), precision=hp, preferred_element_type=F32
            )
            f_ref[z * 128 : (z + 1) * 128, lanes] = listed * src
    for z in range(4):
        resid_ref[z] = f_ref[z * 128 : (z + 1) * 128, :]

    half = lax.broadcasted_iota(jnp.int32, (64, 8, 256), 1) < 4
    nn, nt = ((1,), (0,)), ((1,), (1,))

    def parts_of(ref, passes):
        return [ref[i] for i in range(3 if passes == 6 else 2)]

    def width(passes):
        return 3 if passes == 6 else 2

    def bulk(j, src_of, recv, ssem, rsem):
        def send(step, carry):
            pw, pn = peer(step, w, n)
            pltpu.make_async_remote_copy(
                src_ref=src_of(pn * NW + pw),
                dst_ref=recv.at[j, me],
                send_sem=ssem.at[j],
                recv_sem=rsem.at[j],
                device_id=(pw, pn),
                device_id_type=MESH,
            ).start()
            return carry

        lax.fori_loop(1, ND, send, 0)

    def gather(j, ag, ssem, rsem):
        def send(step, carry):
            pw, pn = peer(step, w, n)
            pltpu.make_async_remote_copy(
                src_ref=ag.at[j, me],
                dst_ref=ag.at[j, me],
                send_sem=ssem.at[j],
                recv_sem=rsem.at[j],
                device_id=(pw, pn),
                device_id_type=MESH,
            ).start()
            return carry

        lax.fori_loop(1, ND, send, 0)

    def wait_others(j, ref, sem):
        part = ref.at[j, pl.ds(0, ND - 1)]
        pltpu.make_async_copy(part, part, sem.at[j]).wait()

    def wait_all(j, ref, sem):
        part = ref.at[j]
        pltpu.make_async_copy(part, part, sem.at[j]).wait()

    def summed(rows):
        return jnp.sum(rows, axis=1, keepdims=True)

    def read_a(j):
        wait_others(j, ag_a, sem_ar)
        wait_others(j, ag_a, sem_as)
        return summed(jnp.sum(ag_a[j], axis=0))

    def one_pass(j, rho):
        first = j == 0
        table = parts_of(tx_ref, FWD)
        s_half = []
        for h in range(2):
            f = split(f_ref[h * 256 : (h + 1) * 256, :], width(FWD))
            s_half.append(product(table, f, nt, FWD).reshape(64, 8, 256))
        sbf[:, 0] = jnp.where(half, s_half[0], pltpu.roll(s_half[1], 4, 1))
        sbf[:, 1] = jnp.where(half, pltpu.roll(s_half[0], 4, 1), s_half[1])
        own = pltpu.make_async_copy(sbf.at[me // 2, me % 2], recvf.at[j, me], sem_fr.at[j])
        own.start()
        bulk(j, lambda p: sbf.at[p // 2, p % 2], recvf, sem_fs, sem_fr)
        gather(j, ag_a, sem_as, sem_ar)
        wait_all(j, recvf, sem_fr)
        table = parts_of(ty_ref, FWD)
        u = []
        for zl in range(2):
            a = jnp.concatenate(
                [
                    recvf[j, q * 32 : (q + 1) * 32, :, zl * 128 : (zl + 1) * 128].reshape(256, 128)
                    for q in range(NN)
                ],
                axis=1,
            )
            u.append(product(split(a, width(FWD)), table, nt, FWD))
        u = jnp.concatenate(u, axis=0)
        v = product(parts_of(b_ref, FWD), split(u, width(FWD)), nn, FWD)
        pi = read_a(j)
        alpha = jnp.where(first, -1.0, rho / pi)
        step = jnp.where(first, 0.0, rho / pi)
        left = c_ref[...] - alpha * v
        c_ref[...] = left
        scaled = left * inv_ref[...]
        q_part = jnp.sum(left * scaled, axis=0, keepdims=True)
        ag_b[j, me] = q_part[:, 0:128] + q_part[:, 128:256] + q_part[:, 256:384] + q_part[:, 384:512]
        back = product(parts_of(bt_ref, INV), split(scaled, width(INV)), nn, INV)
        table = parts_of(ty_ref, INV)
        for zl in range(2):
            r = product(split(back[zl * 256 : (zl + 1) * 256], width(INV)), table, nn, INV)
            for q in range(NN):
                sbi[q * 32 : (q + 1) * 32, :, zl * 128 : (zl + 1) * 128] = r[:, q * 128 : (q + 1) * 128].reshape(32, 8, 128)
        own = pltpu.make_async_copy(sbi.at[me], recvi.at[j, me], sem_ir.at[j])
        own.start()
        bulk(j, lambda p: sbi.at[p], recvi, sem_is, sem_ir)
        gather(j, ag_b, sem_bs, sem_br)
        wait_others(j, recvf, sem_fs)
        wait_all(j, recvi, sem_ir)
        wait_others(j, ag_b, sem_br)
        wait_others(j, ag_b, sem_bs)
        wait_others(j, recvi, sem_is)
        fresh = summed(jnp.sum(ag_b[j], axis=0))
        mix = jnp.where(first, 0.0, fresh / rho)
        got = recvi[j].reshape(64, 2, 8, 256)
        even, odd = got[:, 0], got[:, 1]
        halves = (
            jnp.where(half, even, pltpu.roll(odd, 4, 1)).reshape(ROWS, 256),
            jnp.where(half, pltpu.roll(even, 4, 1), odd).reshape(ROWS, 256),
        )
        table = parts_of(tx_ref, INV)
        for h in range(2):
            r = product(split(halves[h].T, width(INV)), table, nn, INV)
            spad[j, 1 + 2 * h : 3 + 2 * h, 8:136, :] = r.reshape(2, 128, NX)
        field = spad.at[j]
        copies = halo(2 + j, lambda z, y: field.at[(z + 1) if isinstance(z, int) else pl.ds(1, 4), y], 8, lambda z, y: field.at[z, y])
        for copy in copies:
            copy.start()

        def update(g, carry):
            z, i = g // 16, g % 16
            rows = pl.ds(pl.multiple_of(8 * g, 8), 8)
            line = pl.ds(pl.multiple_of(8 * i, 8), 8)
            d = d_ref[rows, :]
            press_ref[z, line, :] = press_ref[z, line, :] + step * d
            resid_ref[z, line, :] = resid_ref[z, line, :] - step * f_ref[rows, :]
            d_ref[rows, :] = spad[j, z + 1, pl.ds(pl.multiple_of(8 + 8 * i, 8), 8), :] + mix * d
            return carry

        lax.fori_loop(0, 64, update, 0)
        for copy in copies:
            copy.wait()

        def stencil(g, carry):
            z, i = g // 16, g % 16
            rows = pl.ds(pl.multiple_of(8 * g, 8), 8)
            c, near = around(field, z, i)
            total = resid_ref[z, pl.ds(pl.multiple_of(8 * i, 8), 8), :] + mix * f_ref[rows, :]
            for q in range(6):
                total = total + wts[q, rows, :] * (c - near[q])
            f_ref[rows, :] = total
            return carry + d_ref[rows, :] * total

        zero = jnp.zeros((8, NX), F32)
        line = jnp.sum(lax.fori_loop(0, 64, stencil, zero), axis=0, keepdims=True)
        ag_a[j + 1, me] = line[:, 0:128] + line[:, 128:256] + line[:, 256:384] + line[:, 384:512]
        return fresh

    rho = lax.fori_loop(0, ITERS, one_pass, jnp.ones((1, 1), F32))
    gather(ITERS, ag_a, sem_as, sem_ar)
    alpha = rho / read_a(ITERS)

    def finish(g, carry):
        z, i = g // 16, g % 16
        rows = pl.ds(pl.multiple_of(8 * g, 8), 8)
        line = pl.ds(pl.multiple_of(8 * i, 8), 8)
        press_ref[z, line, :] = press_ref[z, line, :] + alpha * d_ref[rows, :]
        resid_ref[z, line, :] = resid_ref[z, line, :] - alpha * f_ref[rows, :]
        return carry

    lax.fori_loop(0, 64, finish, 0)


def on_device(temp, phase, table, north, east):
    w = lax.axis_index("wide")
    n = lax.axis_index("narrow")
    me = n * NW + w
    ez = eigen_np(NZ)
    ex = eigen_np(NX).astype(np.float32)
    ey = eigen_np(NY).astype(np.float32)
    own = lax.dynamic_slice(jnp.asarray(ex), (4 * me,), (4,))
    rowden = (jnp.asarray((ez + 0.01).astype(np.float32))[:, None] + own[None, :]).reshape(ROWS, 1)
    colden = jnp.asarray(ey).reshape(1, NY)
    bz = z_table()
    tables = [jnp.asarray(split_np(t)) for t in (cosine_np(NX), cosine_np(NY), bz, bz.T)]
    vmem = pl.BlockSpec(memory_space=pltpu.VMEM)
    smem = pl.BlockSpec(memory_space=pltpu.SMEM)
    shape = jax.ShapeDtypeStruct((4, 128, NX), F32)
    dma = pltpu.SemaphoreType.DMA
    square = pltpu.VMEM((ROWS, NX), F32)
    return pl.pallas_call(
        whole_kernel,
        out_shape=(shape, shape, shape),
        in_specs=[vmem, vmem, smem] + [vmem] * 8,
        out_specs=(vmem, vmem, vmem),
        scratch_shapes=[
            pltpu.VMEM((6, 144, NX), F32),
            pltpu.VMEM((6, 144, NX), jnp.int32),
            pltpu.VMEM((ITERS, 6, 144, NX), F32),
            pltpu.VMEM((6, ROWS, NX), F32),
            square,
            square,
            square,
            square,
            square,
            pltpu.VMEM((64, 2, 8, 256), F32),
            pltpu.VMEM((ND, 8, 256), F32),
            pltpu.VMEM((ITERS, ND, 8, 256), F32),
            pltpu.VMEM((ITERS, ND, 8, 256), F32),
            pltpu.VMEM((ITERS + 1, ND, 1, 128), F32),
            pltpu.VMEM((ITERS, ND, 1, 128), F32),
            dma((ITERS,)),
            dma((ITERS,)),
            dma((ITERS,)),
            dma((ITERS,)),
            dma((ITERS + 1,)),
            dma((ITERS + 1,)),
            dma((ITERS,)),
            dma((ITERS,)),
            dma((5, 4)),
            dma((5, 4)),
        ],
        compiler_params=pltpu.CompilerParams(
            collective_id=0, has_side_effects=True, vmem_limit_bytes=60 * 2**20
        ),
    )(temp, phase, table.reshape(16), north, east, *tables, rowden, colden)


def solution(mesh):
    block = P("wide", "narrow", None)
    return jax.shard_map(
        on_device,
        mesh=mesh,
        in_specs=(block, block, block, P(), P()),
        out_specs=(block, block, block),
        check_vma=False,
    )
```

```python
import functools
import math

import jax
import jax.numpy as jnp
import ml_dtypes
import numpy as np
from jax import lax
from jax.experimental import pallas as pl
from jax.experimental.pallas import tpu as pltpu
from jax.sharding import PartitionSpec as P

MESH = pl.DeviceIdType.MESH
F32 = jnp.float32
BF16 = jnp.bfloat16
NX, NY, NZ = 512, 512, 128
NW, NN = 32, 4
ND = NW * NN
ITERS = 3
ROWS = 512
LINES = 17


def cosine_np(m):
    k = np.arange(m)[:, None]
    i = np.arange(m)[None, :]
    scale = np.where(k == 0, math.sqrt(1.0 / m), math.sqrt(2.0 / m))
    return scale * np.cos(np.pi * ((k * (2 * i + 1)) % (4 * m)) / (2 * m))


def eigen_np(m):
    return 4.0 * np.sin(np.pi * np.arange(m) / (2 * m)) ** 2


def split_np(table):
    parts = []
    rest = table.astype(np.float64)
    for _ in range(2):
        part = rest.astype(np.float32).astype(ml_dtypes.bfloat16)
        parts.append(part)
        rest = rest - part.astype(np.float64)
    return np.stack(parts)


def z_table():
    table = cosine_np(NZ).reshape(NZ, NW, 2, 2).transpose(0, 3, 1, 2)
    big = np.zeros((NZ, 4, 2, NW, 2, 4))
    for k in range(4):
        big[:, k, :, :, :, k] = table
    return big.reshape(ROWS, ROWS)


def split(x):
    high = x.astype(BF16)
    return high, (x - high.astype(F32)).astype(BF16)


def product(a, b, dims):
    total = None
    for i, j in ((0, 1), (1, 0), (0, 0)):
        term = lax.dot_general(a[i], b[j], (dims, ((), ())), preferred_element_type=F32)
        total = term if total is None else total + term
    return total


def peer(step, w, n):
    dx, dy, dz, dc = step % 4, (step // 4) % 4, (step // 16) % 4, step // 64
    y, z, c = w // 8, (w // 2) % 4, w % 2
    return ((y + dy) % 4) * 8 + ((z + dz) % 4) * 2 + (c + dc) % 2, (n + dx) % 4


def whole_kernel(
    temp_ref, phase_ref, table_ref, north_ref, east_ref, tx_ref, ty_ref, b_ref, bt_ref, ez_ref, ey_ref, ex_ref,
    tnext_ref, press_ref, resid_ref,
    tpad, ppad, spad, wts, mass, f_ref, c_ref, d_ref, inv_ref,
    sbf, sbi, recvf, recvi, red_n, red_w,
    sem_fs, sem_fr, sem_is, sem_ir, sem_rs, sem_rr, sem_hs, sem_hr, sem_ready,
):
    w = lax.axis_index("wide")
    n = lax.axis_index("narrow")
    me = n * NW + w

    barrier = pltpu.get_barrier_semaphore()

    def greet_narrow(step, carry):
        pl.semaphore_signal(barrier, inc=1, device_id=(w, (n + step) % NN), device_id_type=MESH)
        return carry

    def greet_wide(step, carry):
        pl.semaphore_signal(barrier, inc=1, device_id=((w + step) % NW, n), device_id_type=MESH)
        return carry

    lax.fori_loop(1, NN, greet_narrow, 0)
    lax.fori_loop(1, NW, greet_wide, 0)

    tpad[1:5, 8:136, :] = temp_ref[...]
    ppad[1:5, 8:136, :] = phase_ref[...]
    lane = lax.broadcasted_iota(jnp.int32, (8, NX), 1)
    own_k = lax.broadcasted_iota(jnp.int32, (8, NX), 0) % 4 + 4 * me
    ex = jnp.sum(jnp.where(lane == own_k, ex_ref[...], 0.0), axis=1, keepdims=True)
    den = ez_ref[...] + ex[None] + ey_ref[...][None]
    inv_ref[...] = (1.0 / den).reshape(ROWS, NX)
    c_ref[...] = jnp.zeros_like(c_ref)
    d_ref[...] = jnp.zeros_like(d_ref)
    press_ref[...] = jnp.zeros_like(press_ref)

    pl.semaphore_wait(barrier, NN - 1 + NW - 1)

    def relay(step, carry):
        pl.semaphore_signal(sem_ready, inc=1, device_id=(w, (n + step) % NN), device_id_type=MESH)
        return carry

    lax.fori_loop(1, NN, relay, 0)

    w_up, w_down = (w + 1) % NW, (w + NW - 1) % NW
    n_up, n_down = (n + 1) % NN, (n + NN - 1) % NN

    def halo(slot, src, at, dst):
        moves = (
            (src(3, pl.ds(at, 128)), dst(0, pl.ds(8, 128)), (w_up, n)),
            (src(0, pl.ds(at, 128)), dst(5, pl.ds(8, 128)), (w_down, n)),
            (src(pl.ds(0, 4), pl.ds(at + 120, 8)), dst(pl.ds(1, 4), pl.ds(0, 8)), (w, n_up)),
            (src(pl.ds(0, 4), pl.ds(at, 8)), dst(pl.ds(1, 4), pl.ds(136, 8)), (w, n_down)),
        )
        copies = []
        for i, (a, b, to) in enumerate(moves):
            copies.append(
                pltpu.make_async_remote_copy(
                    src_ref=a,
                    dst_ref=b,
                    send_sem=sem_hs.at[slot, i],
                    recv_sem=sem_hr.at[slot, i],
                    device_id=to,
                    device_id_type=MESH,
                )
            )
        return copies

    head = halo(0, lambda z, y: temp_ref.at[z, y], 0, lambda z, y: tpad.at[z, y])
    head += halo(1, lambda z, y: phase_ref.at[z, y], 0, lambda z, y: ppad.at[z, y])
    for copy in head:
        copy.start()
    for copy in head:
        copy.wait()

    row8 = lax.broadcasted_iota(jnp.int32, (8, NX), 0)
    lane8 = lax.broadcasted_iota(jnp.int32, (8, NX), 1)

    def around(pad, z, i):
        mid = pl.ds(pl.multiple_of(8 + 8 * i, 8), 8)
        low = pl.ds(pl.multiple_of(8 * i, 8), 8)
        high = pl.ds(pl.multiple_of(16 + 8 * i, 8), 8)
        c = pad[z + 1, mid, :]
        up = pad[z + 1, high, :]
        down = pad[z + 1, low, :]
        near = (
            pad[z + 2, mid, :],
            pad[z, mid, :],
            pltpu.roll(jnp.where(row8 == 0, up, c), 7, 0),
            pltpu.roll(jnp.where(row8 == 7, down, c), 1, 0),
            pltpu.roll(c, NX - 1, 1),
            pltpu.roll(c, 1, 1),
        )
        return c, near

    def head_chunk(g, carry):
        z, i = g // 16, g % 16
        rows = pl.ds(pl.multiple_of(8 * g, 8), 8)
        c, near = around(tpad, z, i)
        pc, pnear = around(ppad, z, i)
        gz = jnp.zeros_like(row8) + (4 * w + z)
        gy = row8 + (n * 128 + 8 * i)
        inside = (gz < NZ - 1, gz > 0, gy < NY - 1, gy > 0, lane8 < NX - 1, lane8 > 0)
        conduct = jnp.where(pc > 0, 1.0, 0.4)
        beta = jnp.where(pc > 0, 1.0, 4.0)
        flux = jnp.zeros_like(c)
        faces = jnp.zeros_like(c)
        for q in range(6):
            ins = jnp.where(inside[q], 1.0, 0.0)
            differ = pnear[q] != pc
            flux = flux + ins * jnp.where(differ, -2.0 * c, near[q] - c)
            faces = faces + ins * jnp.where(differ, 1.0, 0.0)
            wts[q, rows, :] = ins * (0.5 * (beta + jnp.where(pnear[q] > 0, 1.0, 4.0)) - 1.0)
        heated = c + 0.06 * conduct * flux
        tnext_ref[z, pl.ds(pl.multiple_of(8 * i, 8), 8), :] = heated
        mass[rows, :] = 2.0 * conduct * faces * heated
        return carry

    lax.fori_loop(0, 64, head_chunk, 0, unroll=2)
    pl.semaphore_wait(sem_ready, NN - 1)

    ra = lax.broadcasted_iota(jnp.int32, (128, 16), 0)
    ca = lax.broadcasted_iota(jnp.int32, (128, 16), 1)
    pick = jnp.where(ra % 16 == ca, 1.0, 0.0).astype(F32)
    rb = lax.broadcasted_iota(jnp.int32, (128, 128), 0)
    cb = lax.broadcasted_iota(jnp.int32, (128, 128), 1)
    hp = lax.Precision.HIGHEST
    spread = lax.dot_general(pick, north_ref[...], (((1,), (0,)), ((), ())), precision=hp, preferred_element_type=F32)
    spread = lax.dot_general(spread, pick, (((1,), (1,)), ((), ())), precision=hp, preferred_element_type=F32)
    north_all = jnp.where(rb // 16 == cb // 16, spread, 0.0)
    east = east_ref[...]
    for t in range(4):
        lanes = slice(t * 128, (t + 1) * 128)
        across = lax.dot_general(mass[:, lanes], east, (((1,), (1,)), ((), ())), precision=hp, preferred_element_type=F32)
        tile = (rb // 16) * 4 + t
        listed = jnp.zeros((128, 128), F32)
        for e in range(16):
            listed = jnp.where(tile == table_ref[e], 0.3, listed)
        for z in range(4):
            src = lax.dot_general(
                north_all, across[z * 128 : (z + 1) * 128], (((1,), (0,)), ((), ())), precision=hp, preferred_element_type=F32
            )
            f_ref[z * 128 : (z + 1) * 128, lanes] = listed * src
    for z in range(4):
        resid_ref[z] = f_ref[z * 128 : (z + 1) * 128, :]

    half = lax.broadcasted_iota(jnp.int32, (64, 8, 128), 1) < 4
    nn, nt = ((1,), (0,)), ((1,), (1,))

    def parts_of(ref):
        return ref[0], ref[1]

    def bulk(j, src_of, recv, ssem, rsem):
        def send(step, carry):
            pw, pn = peer(step, w, n)
            pltpu.make_async_remote_copy(
                src_ref=src_of(pn * NW + pw),
                dst_ref=recv.at[j, me, pl.ds(0, LINES)],
                send_sem=ssem.at[j],
                recv_sem=rsem.at[j],
                device_id=(pw, pn),
                device_id_type=MESH,
            ).start()
            return carry

        lax.fori_loop(1, ND, send, 0)

    def wait_others(j, ref, sem):
        part = ref.at[j, pl.ds(0, ND - 1), pl.ds(0, LINES)]
        pltpu.make_async_copy(part, part, sem.at[j]).wait()

    def wait_all(j, ref, sem):
        part = ref.at[j, :, pl.ds(0, LINES)]
        pltpu.make_async_copy(part, part, sem.at[j]).wait()

    def folded(line):
        return line[:, 0:128] + line[:, 128:256] + line[:, 256:384] + line[:, 384:512]

    def summed(rows):
        return jnp.sum(rows, axis=1, keepdims=True)

    def one_pass(j, carry):
        rho, line = carry
        first = j == 0
        table = parts_of(tx_ref)
        low = product(table, split(f_ref[0:256, :]), nt)
        high = product(table, split(f_ref[256:512, :]), nt)
        for zl in range(2):
            a = low[:, zl * 128 : (zl + 1) * 128].reshape(64, 8, 128)
            b = high[:, zl * 128 : (zl + 1) * 128].reshape(64, 8, 128)
            sbf[:, 0, zl * 8 : (zl + 1) * 8, :] = jnp.where(half, a, pltpu.roll(b, 4, 1))
            sbf[:, 1, zl * 8 : (zl + 1) * 8, :] = jnp.where(half, pltpu.roll(a, 4, 1), b)
        sbf[:, :, 16:17, :] = jnp.broadcast_to(line, (64, 2, 1, 128))
        sent = pl.ds(0, LINES)
        own = pltpu.make_async_copy(sbf.at[me // 2, me % 2, sent], recvf.at[j, me, sent], sem_fr.at[j])
        own.start()
        bulk(j, lambda p: sbf.at[p // 2, p % 2, sent], recvf, sem_fs, sem_fr)
        wait_all(j, recvf, sem_fr)
        table = parts_of(ty_ref)
        u = []
        for zl in range(2):
            a = jnp.concatenate(
                [
                    recvf[j, q * 32 : (q + 1) * 32, zl * 8 : (zl + 1) * 8, :].reshape(256, 128)
                    for q in range(NN)
                ],
                axis=1,
            )
            u.append(product(split(a), table, nt))
        u = jnp.concatenate(u, axis=0)
        v = product(parts_of(b_ref), split(u), nn)
        pi = summed(jnp.sum(recvf[j, :, 16:17, :], axis=0))
        alpha = jnp.where(first, -1.0, rho / pi)
        step = jnp.where(first, 0.0, rho / pi)
        left = c_ref[...] - alpha * v
        c_ref[...] = left
        scaled = left * inv_ref[...]
        q_part = jnp.sum(left * scaled, axis=0, keepdims=True)
        sbi[:, 16:17, :] = jnp.broadcast_to(folded(q_part), (ND, 1, 128))
        back = product(parts_of(bt_ref), split(scaled), nn)
        table = parts_of(ty_ref)
        for zl in range(2):
            r = product(split(back[zl * 256 : (zl + 1) * 256]), table, nn)
            for q in range(NN):
                sbi[q * 32 : (q + 1) * 32, zl * 8 : (zl + 1) * 8, :] = r[:, q * 128 : (q + 1) * 128].reshape(32, 8, 128)
        own = pltpu.make_async_copy(sbi.at[me, sent], recvi.at[j, me, sent], sem_ir.at[j])
        own.start()
        bulk(j, lambda p: sbi.at[p, sent], recvi, sem_is, sem_ir)
        wait_others(j, recvf, sem_fs)
        wait_all(j, recvi, sem_ir)
        wait_others(j, recvi, sem_is)
        fresh = summed(jnp.sum(recvi[j, :, 16:17, :], axis=0))
        mix = jnp.where(first, 0.0, fresh / rho)
        planes = [[], []]
        for zl in range(2):
            got = recvi[j, :, zl * 8 : (zl + 1) * 8, :].reshape(64, 2, 8, 128)
            even, odd = got[:, 0], got[:, 1]
            planes[0].append(jnp.where(half, even, pltpu.roll(odd, 4, 1)).reshape(ROWS, 128).T)
            planes[1].append(jnp.where(half, pltpu.roll(even, 4, 1), odd).reshape(ROWS, 128).T)
        table = parts_of(tx_ref)
        for h in range(2):
            r = product(split(jnp.concatenate(planes[h], axis=0)), table, nn)
            spad[j, 1 + 2 * h : 3 + 2 * h, 8:136, :] = r.reshape(2, 128, NX)
        field = spad.at[j]
        copies = halo(2 + j, lambda z, y: field.at[(z + 1) if isinstance(z, int) else pl.ds(1, 4), y], 8, lambda z, y: field.at[z, y])
        for copy in copies:
            copy.start()

        def update(g, carry):
            z, i = g // 16, g % 16
            rows = pl.ds(pl.multiple_of(8 * g, 8), 8)
            line = pl.ds(pl.multiple_of(8 * i, 8), 8)
            d = d_ref[rows, :]
            press_ref[z, line, :] = press_ref[z, line, :] + step * d
            resid_ref[z, line, :] = resid_ref[z, line, :] - step * f_ref[rows, :]
            d_ref[rows, :] = spad[j, z + 1, pl.ds(pl.multiple_of(8 + 8 * i, 8), 8), :] + mix * d
            return carry

        lax.fori_loop(0, 64, update, 0, unroll=4)
        for copy in copies:
            copy.wait()

        def stencil(g, carry):
            z, i = g // 16, g % 16
            rows = pl.ds(pl.multiple_of(8 * g, 8), 8)
            c, near = around(field, z, i)
            total = resid_ref[z, pl.ds(pl.multiple_of(8 * i, 8), 8), :] + mix * f_ref[rows, :]
            for q in range(6):
                total = total + wts[q, rows, :] * (c - near[q])
            f_ref[rows, :] = total
            return carry + d_ref[rows, :] * total

        zero = jnp.zeros((8, NX), F32)
        line = jnp.sum(lax.fori_loop(0, 64, stencil, zero, unroll=2), axis=0, keepdims=True)
        return fresh, folded(line)

    rho, line = lax.fori_loop(0, ITERS, one_pass, (jnp.ones((1, 1), F32), jnp.ones((1, 128), F32)))

    def gather(slots, slot, count, to, ssem, rsem):
        def send(step, carry):
            pltpu.make_async_remote_copy(
                src_ref=slots.at[slot],
                dst_ref=slots.at[slot],
                send_sem=ssem,
                recv_sem=rsem,
                device_id=to(step),
                device_id_type=MESH,
            ).start()
            return carry

        lax.fori_loop(1, count, send, 0)
        part = slots.at[pl.ds(0, count - 1)]
        pltpu.make_async_copy(part, part, rsem).wait()
        pltpu.make_async_copy(part, part, ssem).wait()
        return jnp.sum(slots[...], axis=0)

    red_n[n] = line
    red_w[w] = gather(red_n, n, NN, lambda step: (w, (n + step) % NN), sem_rs.at[0], sem_rr.at[0])
    pi = summed(gather(red_w, w, NW, lambda step: ((w + step) % NW, n), sem_rs.at[1], sem_rr.at[1]))
    alpha = rho / pi

    def finish(g, carry):
        z, i = g // 16, g % 16
        rows = pl.ds(pl.multiple_of(8 * g, 8), 8)
        line = pl.ds(pl.multiple_of(8 * i, 8), 8)
        press_ref[z, line, :] = press_ref[z, line, :] + alpha * d_ref[rows, :]
        resid_ref[z, line, :] = resid_ref[z, line, :] - alpha * f_ref[rows, :]
        return carry

    lax.fori_loop(0, 64, finish, 0, unroll=4)


def on_device(temp, phase, table, north, east):
    ez = np.repeat(eigen_np(NZ) + 0.01, 4).reshape(64, 8, 1).astype(np.float32)
    ey = eigen_np(NY).astype(np.float32).reshape(1, NY)
    ex = eigen_np(NX).astype(np.float32).reshape(1, NX)
    bz = z_table()
    tables = [jnp.asarray(split_np(t)) for t in (cosine_np(NX), cosine_np(NY), bz, bz.T)]
    vmem = pl.BlockSpec(memory_space=pltpu.VMEM)
    smem = pl.BlockSpec(memory_space=pltpu.SMEM)
    shape = jax.ShapeDtypeStruct((4, 128, NX), F32)
    dma = pltpu.SemaphoreType.DMA
    square = pltpu.VMEM((ROWS, NX), F32)
    return pl.pallas_call(
        whole_kernel,
        out_shape=(shape, shape, shape),
        in_specs=[vmem, vmem, smem] + [vmem] * 9,
        out_specs=(vmem, vmem, vmem),
        scratch_shapes=[
            pltpu.VMEM((6, 144, NX), F32),
            pltpu.VMEM((6, 144, NX), jnp.int32),
            pltpu.VMEM((ITERS, 6, 144, NX), F32),
            pltpu.VMEM((6, ROWS, NX), F32),
            square,
            square,
            square,
            square,
            square,
            pltpu.VMEM((64, 2, 24, 128), F32),
            pltpu.VMEM((ND, 24, 128), F32),
            pltpu.VMEM((ITERS, ND, 24, 128), F32),
            pltpu.VMEM((ITERS, ND, 24, 128), F32),
            pltpu.VMEM((NN, 1, 128), F32),
            pltpu.VMEM((NW, 1, 128), F32),
            dma((ITERS,)),
            dma((ITERS,)),
            dma((ITERS,)),
            dma((ITERS,)),
            dma((2,)),
            dma((2,)),
            dma((5, 4)),
            dma((5, 4)),
            pltpu.SemaphoreType.REGULAR,
        ],
        compiler_params=pltpu.CompilerParams(
            collective_id=0, has_side_effects=True, vmem_limit_bytes=60 * 2**20
        ),
    )(temp, phase, table.reshape(16), north, east, *tables, jnp.asarray(ez), jnp.asarray(ey), jnp.asarray(ex))


def solution(mesh):
    block = P("wide", "narrow", None)
    return jax.shard_map(
        on_device,
        mesh=mesh,
        in_specs=(block, block, block, P(), P()),
        out_specs=(block, block, block),
        check_vma=False,
    )
```

```python
import functools
import math

import jax
import jax.numpy as jnp
import ml_dtypes
import numpy as np
from jax import lax
from jax.experimental import pallas as pl
from jax.experimental.pallas import tpu as pltpu
from jax.sharding import PartitionSpec as P

MESH = pl.DeviceIdType.MESH
F32 = jnp.float32
BF16 = jnp.bfloat16
NX, NY, NZ = 512, 512, 128
NW, NN = 32, 4
ND = NW * NN
ITERS = 3
ROWS = 512
LINES = 17


def cosine_np(m):
    k = np.arange(m)[:, None]
    i = np.arange(m)[None, :]
    scale = np.where(k == 0, math.sqrt(1.0 / m), math.sqrt(2.0 / m))
    return scale * np.cos(np.pi * ((k * (2 * i + 1)) % (4 * m)) / (2 * m))


def eigen_np(m):
    return 4.0 * np.sin(np.pi * np.arange(m) / (2 * m)) ** 2


def split_np(table):
    parts = []
    rest = table.astype(np.float64)
    for _ in range(2):
        part = rest.astype(np.float32).astype(ml_dtypes.bfloat16)
        parts.append(part)
        rest = rest - part.astype(np.float64)
    return np.stack(parts)


def z_table():
    table = cosine_np(NZ).reshape(NZ, NW, 2, 2).transpose(0, 3, 1, 2)
    big = np.zeros((NZ, 4, 2, NW, 2, 4))
    for k in range(4):
        big[:, k, :, :, :, k] = table
    return big.reshape(ROWS, ROWS)


def split(x):
    high = x.astype(BF16)
    return high, (x - high.astype(F32)).astype(BF16)


def product(a, b, dims):
    total = None
    for i, j in ((0, 1), (1, 0), (0, 0)):
        term = lax.dot_general(a[i], b[j], (dims, ((), ())), preferred_element_type=F32)
        total = term if total is None else total + term
    return total


HOPS = sorted(np.ndindex(3, 3, 3), key=lambda hops: -sum(hops))


def each_peer(w, n, send):
    y, z, c = w // 8, (w // 2) % 4, w % 2
    for hops in HOPS:
        ones = sum(h == 1 for h in hops)

        def body(turn, carry, hops=hops):
            flip, rest = turn % 2, turn // 2
            offset = []
            for h in hops:
                if h == 1:
                    offset.append(1 + 2 * (rest % 2))
                    rest = rest // 2
                else:
                    offset.append(h)
            dx, dy, dz = offset
            send(((y + dy) % 4) * 8 + ((z + dz) % 4) * 2 + (c + flip) % 2, (n + dx) % 4)
            return carry

        lax.fori_loop(1 if sum(hops) == 0 else 0, 2 ** (ones + 1), body, 0)


def whole_kernel(
    temp_ref, phase_ref, table_ref, north_ref, east_ref, tx_any, ty_any, b_any, bt_any, ez_ref, ey_ref, ex_ref,
    tnext_ref, press_ref, resid_ref,
    tx_ref, ty_ref, b_ref, bt_ref, tpad, ppad, spad, wts, mass, f_ref, c_ref, d_ref, inv_ref,
    sbf, sbi, recvf, recvi, red_n, red_w,
    sem_fs, sem_fr, sem_is, sem_ir, sem_rs, sem_rr, sem_hs, sem_hr, sem_ready, sem_load,
):
    w = lax.axis_index("wide")
    n = lax.axis_index("narrow")
    me = n * NW + w

    barrier = pltpu.get_barrier_semaphore()
    loads = [
        pltpu.make_async_copy(a, b, sem_load.at[i])
        for i, (a, b) in enumerate(
            (
                (temp_ref, tpad.at[pl.ds(1, 4), pl.ds(8, 128)]),
                (phase_ref, ppad.at[pl.ds(1, 4), pl.ds(8, 128)]),
                (tx_any, tx_ref),
                (ty_any, ty_ref),
                (b_any, b_ref),
                (bt_any, bt_ref),
            )
        )
    ]
    for load in loads:
        load.start()

    def greet_narrow(step, carry):
        pl.semaphore_signal(barrier, inc=1, device_id=(w, (n + step) % NN), device_id_type=MESH)
        return carry

    def greet_wide(step, carry):
        pl.semaphore_signal(barrier, inc=1, device_id=((w + step) % NW, n), device_id_type=MESH)
        return carry

    lax.fori_loop(1, NN, greet_narrow, 0)
    lax.fori_loop(1, NW, greet_wide, 0)

    pl.semaphore_wait(barrier, NN - 1 + NW - 1)

    def relay(step, carry):
        pl.semaphore_signal(sem_ready, inc=1, device_id=(w, (n + step) % NN), device_id_type=MESH)
        return carry

    lax.fori_loop(1, NN, relay, 0)

    w_up, w_down = (w + 1) % NW, (w + NW - 1) % NW
    n_up, n_down = (n + 1) % NN, (n + NN - 1) % NN

    def halo(slot, src, at, dst):
        moves = (
            (src(3, pl.ds(at, 128)), dst(0, pl.ds(8, 128)), (w_up, n)),
            (src(0, pl.ds(at, 128)), dst(5, pl.ds(8, 128)), (w_down, n)),
            (src(pl.ds(0, 4), pl.ds(at + 120, 8)), dst(pl.ds(1, 4), pl.ds(0, 8)), (w, n_up)),
            (src(pl.ds(0, 4), pl.ds(at, 8)), dst(pl.ds(1, 4), pl.ds(136, 8)), (w, n_down)),
        )
        copies = []
        for i, (a, b, to) in enumerate(moves):
            copies.append(
                pltpu.make_async_remote_copy(
                    src_ref=a,
                    dst_ref=b,
                    send_sem=sem_hs.at[slot, i],
                    recv_sem=sem_hr.at[slot, i],
                    device_id=to,
                    device_id_type=MESH,
                )
            )
        return copies

    head = halo(0, lambda z, y: temp_ref.at[z, y], 0, lambda z, y: tpad.at[z, y])
    head += halo(1, lambda z, y: phase_ref.at[z, y], 0, lambda z, y: ppad.at[z, y])
    for copy in head:
        copy.start()
    lane = lax.broadcasted_iota(jnp.int32, (8, NX), 1)
    own_k = lax.broadcasted_iota(jnp.int32, (8, NX), 0) % 4 + 4 * me
    ex = jnp.sum(jnp.where(lane == own_k, ex_ref[...], 0.0), axis=1, keepdims=True)
    den = ez_ref[...] + ex[None] + ey_ref[...][None]
    inv_ref[...] = (1.0 / den).reshape(ROWS, NX)
    c_ref[...] = jnp.zeros_like(c_ref)
    d_ref[...] = jnp.zeros_like(d_ref)
    press_ref[...] = jnp.zeros_like(press_ref)
    for load in loads:
        load.wait()

    row8 = lax.broadcasted_iota(jnp.int32, (8, NX), 0)
    lane8 = lax.broadcasted_iota(jnp.int32, (8, NX), 1)

    def around(pad, z, i):
        mid = pl.ds(pl.multiple_of(8 + 8 * i, 8), 8)
        low = pl.ds(pl.multiple_of(8 * i, 8), 8)
        high = pl.ds(pl.multiple_of(16 + 8 * i, 8), 8)
        c = pad[z + 1, mid, :]
        up = pad[z + 1, high, :]
        down = pad[z + 1, low, :]
        near = (
            pad[z + 2, mid, :],
            pad[z, mid, :],
            pltpu.roll(jnp.where(row8 == 0, up, c), 7, 0),
            pltpu.roll(jnp.where(row8 == 7, down, c), 1, 0),
            pltpu.roll(c, NX - 1, 1),
            pltpu.roll(c, 1, 1),
        )
        return c, near

    def sweep(copies, body, carry):
        carry = lax.fori_loop(0, 28, lambda q, c: body(1 + q // 14, 1 + q % 14, c), carry, unroll=2)
        copies[2].wait()
        copies[3].wait()
        carry = lax.fori_loop(0, 4, lambda q, c: body(1 + q // 2, 15 * (q % 2), c), carry)
        copies[0].wait()
        copies[1].wait()
        return lax.fori_loop(0, 32, lambda q, c: body(3 * (q // 16), q % 16, c), carry, unroll=2)

    class Both:
        def __init__(self, a, b):
            self.pair = (a, b)

        def wait(self):
            for copy in self.pair:
                copy.wait()

    def head_chunk(z, i, carry):
        rows = pl.ds(pl.multiple_of(8 * (16 * z + i), 8), 8)
        c, near = around(tpad, z, i)
        pc, pnear = around(ppad, z, i)
        gz = jnp.zeros_like(row8) + (4 * w + z)
        gy = row8 + (n * 128 + 8 * i)
        inside = (gz < NZ - 1, gz > 0, gy < NY - 1, gy > 0, lane8 < NX - 1, lane8 > 0)
        conduct = jnp.where(pc > 0, 1.0, 0.4)
        beta = jnp.where(pc > 0, 1.0, 4.0)
        flux = jnp.zeros_like(c)
        faces = jnp.zeros_like(c)
        for q in range(6):
            ins = jnp.where(inside[q], 1.0, 0.0)
            differ = pnear[q] != pc
            flux = flux + ins * jnp.where(differ, -2.0 * c, near[q] - c)
            faces = faces + ins * jnp.where(differ, 1.0, 0.0)
            wts[q, rows, :] = ins * (0.5 * (beta + jnp.where(pnear[q] > 0, 1.0, 4.0)) - 1.0)
        heated = c + 0.06 * conduct * flux
        tnext_ref[z, pl.ds(pl.multiple_of(8 * i, 8), 8), :] = heated
        mass[rows, :] = 2.0 * conduct * faces * heated
        return carry

    sweep([Both(head[i], head[4 + i]) for i in range(4)], head_chunk, 0)
    pl.semaphore_wait(sem_ready, NN - 1)

    ra = lax.broadcasted_iota(jnp.int32, (128, 16), 0)
    ca = lax.broadcasted_iota(jnp.int32, (128, 16), 1)
    pick = jnp.where(ra % 16 == ca, 1.0, 0.0).astype(F32)
    rb = lax.broadcasted_iota(jnp.int32, (128, 128), 0)
    cb = lax.broadcasted_iota(jnp.int32, (128, 128), 1)
    hp = lax.Precision.HIGHEST
    spread = lax.dot_general(pick, north_ref[...], (((1,), (0,)), ((), ())), precision=hp, preferred_element_type=F32)
    spread = lax.dot_general(spread, pick, (((1,), (1,)), ((), ())), precision=hp, preferred_element_type=F32)
    north_all = jnp.where(rb // 16 == cb // 16, spread, 0.0)
    east = east_ref[...]
    for t in range(4):
        lanes = slice(t * 128, (t + 1) * 128)
        across = lax.dot_general(mass[:, lanes], east, (((1,), (1,)), ((), ())), precision=hp, preferred_element_type=F32)
        tile = (rb // 16) * 4 + t
        listed = jnp.zeros((128, 128), F32)
        for e in range(16):
            listed = jnp.where(tile == table_ref[e], 0.3, listed)
        for z in range(4):
            src = lax.dot_general(
                north_all, across[z * 128 : (z + 1) * 128], (((1,), (0,)), ((), ())), precision=hp, preferred_element_type=F32
            )
            f_ref[z * 128 : (z + 1) * 128, lanes] = listed * src
    for z in range(4):
        resid_ref[z] = f_ref[z * 128 : (z + 1) * 128, :]

    half = lax.broadcasted_iota(jnp.int32, (64, 8, 128), 1) < 4
    nn, nt = ((1,), (0,)), ((1,), (1,))

    def parts_of(ref):
        return ref[0], ref[1]

    def bulk(j, src_of, recv, ssem, rsem):
        def send(pw, pn):
            pltpu.make_async_remote_copy(
                src_ref=src_of(pn * NW + pw),
                dst_ref=recv.at[j, me, pl.ds(0, LINES)],
                send_sem=ssem.at[j],
                recv_sem=rsem.at[j],
                device_id=(pw, pn),
                device_id_type=MESH,
            ).start()

        each_peer(w, n, send)

    def wait_others(j, ref, sem):
        part = ref.at[j, pl.ds(0, ND - 1), pl.ds(0, LINES)]
        pltpu.make_async_copy(part, part, sem.at[j]).wait()

    def wait_all(j, ref, sem):
        part = ref.at[j, :, pl.ds(0, LINES)]
        pltpu.make_async_copy(part, part, sem.at[j]).wait()

    def folded(line):
        return line[:, 0:128] + line[:, 128:256] + line[:, 256:384] + line[:, 384:512]

    def summed(rows):
        return jnp.sum(rows, axis=1, keepdims=True)

    def one_pass(j, carry):
        rho, line = carry
        first = j == 0
        table = parts_of(tx_ref)
        low = product(table, split(f_ref[0:256, :]), nt)
        high = product(table, split(f_ref[256:512, :]), nt)
        for zl in range(2):
            a = low[:, zl * 128 : (zl + 1) * 128].reshape(64, 8, 128)
            b = high[:, zl * 128 : (zl + 1) * 128].reshape(64, 8, 128)
            sbf[:, 0, zl * 8 : (zl + 1) * 8, :] = jnp.where(half, a, pltpu.roll(b, 4, 1))
            sbf[:, 1, zl * 8 : (zl + 1) * 8, :] = jnp.where(half, pltpu.roll(a, 4, 1), b)
        sbf[:, :, 16:17, :] = jnp.broadcast_to(line, (64, 2, 1, 128))
        sent = pl.ds(0, LINES)
        own = pltpu.make_async_copy(sbf.at[me // 2, me % 2, sent], recvf.at[j, me, sent], sem_fr.at[j])
        own.start()
        bulk(j, lambda p: sbf.at[p // 2, p % 2, sent], recvf, sem_fs, sem_fr)
        wait_all(j, recvf, sem_fr)
        table = parts_of(ty_ref)
        u = []
        for zl in range(2):
            a = jnp.concatenate(
                [
                    recvf[j, q * 32 : (q + 1) * 32, zl * 8 : (zl + 1) * 8, :].reshape(256, 128)
                    for q in range(NN)
                ],
                axis=1,
            )
            u.append(product(split(a), table, nt))
        u = jnp.concatenate(u, axis=0)
        v = product(parts_of(b_ref), split(u), nn)
        pi = summed(jnp.sum(recvf[j, :, 16:17, :], axis=0))
        alpha = jnp.where(first, -1.0, rho / pi)
        step = jnp.where(first, 0.0, rho / pi)
        left = c_ref[...] - alpha * v
        c_ref[...] = left
        scaled = left * inv_ref[...]
        q_part = jnp.sum(left * scaled, axis=0, keepdims=True)
        sbi[:, 16:17, :] = jnp.broadcast_to(folded(q_part), (ND, 1, 128))
        back = product(parts_of(bt_ref), split(scaled), nn)
        table = parts_of(ty_ref)
        for zl in range(2):
            r = product(split(back[zl * 256 : (zl + 1) * 256]), table, nn)
            for q in range(NN):
                sbi[q * 32 : (q + 1) * 32, zl * 8 : (zl + 1) * 8, :] = r[:, q * 128 : (q + 1) * 128].reshape(32, 8, 128)
        own = pltpu.make_async_copy(sbi.at[me, sent], recvi.at[j, me, sent], sem_ir.at[j])
        own.start()
        bulk(j, lambda p: sbi.at[p, sent], recvi, sem_is, sem_ir)

        def update(g, carry):
            z, i = g // 16, g % 16
            rows = pl.ds(pl.multiple_of(8 * g, 8), 8)
            line = pl.ds(pl.multiple_of(8 * i, 8), 8)
            press_ref[z, line, :] = press_ref[z, line, :] + step * d_ref[rows, :]
            resid_ref[z, line, :] = resid_ref[z, line, :] - step * f_ref[rows, :]
            return carry

        lax.fori_loop(0, 64, update, 0, unroll=4)
        wait_others(j, recvf, sem_fs)
        wait_all(j, recvi, sem_ir)
        wait_others(j, recvi, sem_is)
        fresh = summed(jnp.sum(recvi[j, :, 16:17, :], axis=0))
        mix = jnp.where(first, 0.0, fresh / rho)
        planes = [[], []]
        for zl in range(2):
            got = recvi[j, :, zl * 8 : (zl + 1) * 8, :].reshape(64, 2, 8, 128)
            even, odd = got[:, 0], got[:, 1]
            planes[0].append(jnp.where(half, even, pltpu.roll(odd, 4, 1)).reshape(ROWS, 128).T)
            planes[1].append(jnp.where(half, pltpu.roll(even, 4, 1), odd).reshape(ROWS, 128).T)
        table = parts_of(tx_ref)
        field = spad.at[j]
        copies = halo(2 + j, lambda z, y: field.at[(z + 1) if isinstance(z, int) else pl.ds(1, 4), y], 8, lambda z, y: field.at[z, y])
        for h in range(2):
            r = product(split(jnp.concatenate(planes[h], axis=0)), table, nn)
            spad[j, 1 + 2 * h : 3 + 2 * h, 8:136, :] = r.reshape(2, 128, NX)
            if h == 0:
                copies[1].start()
        copies[0].start()
        copies[2].start()
        copies[3].start()

        def stencil(z, i, carry):
            rows = pl.ds(pl.multiple_of(8 * (16 * z + i), 8), 8)
            c, near = around(field, z, i)
            total = resid_ref[z, pl.ds(pl.multiple_of(8 * i, 8), 8), :] + mix * f_ref[rows, :]
            for q in range(6):
                total = total + wts[q, rows, :] * (c - near[q])
            f_ref[rows, :] = total
            d = c + mix * d_ref[rows, :]
            d_ref[rows, :] = d
            return carry + d * total

        line = jnp.sum(sweep(copies, stencil, jnp.zeros((8, NX), F32)), axis=0, keepdims=True)
        return fresh, folded(line)

    rho, line = lax.fori_loop(0, ITERS, one_pass, (jnp.ones((1, 1), F32), jnp.ones((1, 128), F32)))

    def gather(slots, slot, count, to, ssem, rsem):
        def send(step, carry):
            pltpu.make_async_remote_copy(
                src_ref=slots.at[slot],
                dst_ref=slots.at[slot],
                send_sem=ssem,
                recv_sem=rsem,
                device_id=to(step),
                device_id_type=MESH,
            ).start()
            return carry

        lax.fori_loop(1, count, send, 0)
        part = slots.at[pl.ds(0, count - 1)]
        pltpu.make_async_copy(part, part, rsem).wait()
        pltpu.make_async_copy(part, part, ssem).wait()
        return jnp.sum(slots[...], axis=0)

    red_n[n] = line
    red_w[w] = gather(red_n, n, NN, lambda step: (w, (n + step) % NN), sem_rs.at[0], sem_rr.at[0])
    pi = summed(gather(red_w, w, NW, lambda step: ((w + step) % NW, n), sem_rs.at[1], sem_rr.at[1]))
    alpha = rho / pi

    def finish(g, carry):
        z, i = g // 16, g % 16
        rows = pl.ds(pl.multiple_of(8 * g, 8), 8)
        line = pl.ds(pl.multiple_of(8 * i, 8), 8)
        press_ref[z, line, :] = press_ref[z, line, :] + alpha * d_ref[rows, :]
        resid_ref[z, line, :] = resid_ref[z, line, :] - alpha * f_ref[rows, :]
        return carry

    lax.fori_loop(0, 64, finish, 0, unroll=4)


def on_device(temp, phase, table, north, east):
    ez = np.repeat(eigen_np(NZ) + 0.01, 4).reshape(64, 8, 1).astype(np.float32)
    ey = eigen_np(NY).astype(np.float32).reshape(1, NY)
    ex = eigen_np(NX).astype(np.float32).reshape(1, NX)
    bz = z_table()
    tables = [jnp.asarray(split_np(t)) for t in (cosine_np(NX), cosine_np(NY), bz, bz.T)]
    vmem = pl.BlockSpec(memory_space=pltpu.VMEM)
    anywhere = pl.BlockSpec(memory_space=pl.ANY)
    tabled = pltpu.VMEM((2, ROWS, ROWS), BF16)
    smem = pl.BlockSpec(memory_space=pltpu.SMEM)
    shape = jax.ShapeDtypeStruct((4, 128, NX), F32)
    dma = pltpu.SemaphoreType.DMA
    square = pltpu.VMEM((ROWS, NX), F32)
    return pl.pallas_call(
        whole_kernel,
        out_shape=(shape, shape, shape),
        in_specs=[anywhere, anywhere, smem, vmem, vmem] + [anywhere] * 4 + [vmem] * 3,
        out_specs=(vmem, vmem, vmem),
        scratch_shapes=[
            tabled,
            tabled,
            tabled,
            tabled,
            pltpu.VMEM((6, 144, NX), F32),
            pltpu.VMEM((6, 144, NX), jnp.int32),
            pltpu.VMEM((ITERS, 6, 144, NX), F32),
            pltpu.VMEM((6, ROWS, NX), F32),
            square,
            square,
            square,
            square,
            square,
            pltpu.VMEM((64, 2, 24, 128), F32),
            pltpu.VMEM((ND, 24, 128), F32),
            pltpu.VMEM((ITERS, ND, 24, 128), F32),
            pltpu.VMEM((ITERS, ND, 24, 128), F32),
            pltpu.VMEM((NN, 1, 128), F32),
            pltpu.VMEM((NW, 1, 128), F32),
            dma((ITERS,)),
            dma((ITERS,)),
            dma((ITERS,)),
            dma((ITERS,)),
            dma((2,)),
            dma((2,)),
            dma((5, 4)),
            dma((5, 4)),
            pltpu.SemaphoreType.REGULAR,
            dma((6,)),
        ],
        compiler_params=pltpu.CompilerParams(
            collective_id=0, has_side_effects=True, vmem_limit_bytes=60 * 2**20
        ),
    )(temp, phase, table.reshape(16), north, east, *tables, jnp.asarray(ez), jnp.asarray(ey), jnp.asarray(ex))


def solution(mesh):
    block = P("wide", "narrow", None)
    return jax.shard_map(
        on_device,
        mesh=mesh,
        in_specs=(block, block, block, P(), P()),
        out_specs=(block, block, block),
        check_vma=False,
    )
```

```python
import functools
import math

import jax
import jax.numpy as jnp
import ml_dtypes
import numpy as np
from jax import lax
from jax.experimental import pallas as pl
from jax.experimental.pallas import tpu as pltpu
from jax.sharding import PartitionSpec as P

MESH = pl.DeviceIdType.MESH
F32 = jnp.float32
BF16 = jnp.bfloat16
NX, NY, NZ = 512, 512, 128
NW, NN = 32, 4
ND = NW * NN
ITERS = 3
ROWS = 512
LINES = 17


def cosine_np(m):
    k = np.arange(m)[:, None]
    i = np.arange(m)[None, :]
    scale = np.where(k == 0, math.sqrt(1.0 / m), math.sqrt(2.0 / m))
    return scale * np.cos(np.pi * ((k * (2 * i + 1)) % (4 * m)) / (2 * m))


def eigen_np(m):
    return 4.0 * np.sin(np.pi * np.arange(m) / (2 * m)) ** 2


def split_np(table):
    parts = []
    rest = table.astype(np.float64)
    for _ in range(2):
        part = rest.astype(np.float32).astype(ml_dtypes.bfloat16)
        parts.append(part)
        rest = rest - part.astype(np.float64)
    return np.stack(parts)


def z_table():
    table = cosine_np(NZ)[:, 0::2].reshape(NZ // 2, 2, NZ // 2)
    big = np.zeros((2, NZ // 2, 4, NZ // 2, 4))
    for k in range(4):
        big[:, :, k, :, k] = table.transpose(1, 0, 2)
    return big.reshape(2, 256, 256)


def split(x):
    high = x.astype(BF16)
    return high, (x - high.astype(F32)).astype(BF16)


def product(a, b, dims):
    total = None
    for i, j in ((0, 1), (1, 0), (0, 0)):
        term = lax.dot_general(a[i], b[j], (dims, ((), ())), preferred_element_type=F32)
        total = term if total is None else total + term
    return total


HOPS = sorted(np.ndindex(3, 3, 3), key=lambda hops: -sum(hops))


def each_peer(w, n, send):
    y, z, c = w // 8, (w // 2) % 4, w % 2
    for hops in HOPS:
        ones = sum(h == 1 for h in hops)

        def body(turn, carry, hops=hops):
            flip, rest = turn % 2, turn // 2
            offset = []
            for h in hops:
                if h == 1:
                    offset.append(1 + 2 * (rest % 2))
                    rest = rest // 2
                else:
                    offset.append(h)
            dx, dy, dz = offset
            send(((y + dy) % 4) * 8 + ((z + dz) % 4) * 2 + (c + flip) % 2, (n + dx) % 4)
            return carry

        lax.fori_loop(1 if sum(hops) == 0 else 0, 2 ** (ones + 1), body, 0)


def whole_kernel(
    temp_ref, phase_ref, table_ref, north_ref, east_ref, tx_any, ty_any, b_any, bt_any, ez_ref, ey_ref, ex_ref,
    tnext_ref, press_ref, resid_ref,
    tx_ref, ty_ref, b_ref, bt_ref, tpad, ppad, spad, wts, mass, f_ref, c_ref, d_ref, inv_ref,
    sbf, sbi, recvf, recvi, red_n, red_w,
    sem_fs, sem_fr, sem_is, sem_ir, sem_rs, sem_rr, sem_hs, sem_hr, sem_ready, sem_load,
):
    w = lax.axis_index("wide")
    n = lax.axis_index("narrow")
    me = n * NW + w

    barrier = pltpu.get_barrier_semaphore()
    loads = [
        pltpu.make_async_copy(a, b, sem_load.at[i])
        for i, (a, b) in enumerate(
            (
                (temp_ref, tpad.at[pl.ds(1, 4), pl.ds(8, 128)]),
                (phase_ref, ppad.at[pl.ds(1, 4), pl.ds(8, 128)]),
                (tx_any, tx_ref),
                (ty_any, ty_ref),
                (b_any, b_ref),
                (bt_any, bt_ref),
            )
        )
    ]
    for load in loads:
        load.start()

    def greet_narrow(step, carry):
        pl.semaphore_signal(barrier, inc=1, device_id=(w, (n + step) % NN), device_id_type=MESH)
        return carry

    def greet_wide(step, carry):
        pl.semaphore_signal(barrier, inc=1, device_id=((w + step) % NW, n), device_id_type=MESH)
        return carry

    lax.fori_loop(1, NN, greet_narrow, 0)
    lax.fori_loop(1, NW, greet_wide, 0)

    pl.semaphore_wait(barrier, NN - 1 + NW - 1)

    def relay(step, carry):
        pl.semaphore_signal(sem_ready, inc=1, device_id=(w, (n + step) % NN), device_id_type=MESH)
        return carry

    lax.fori_loop(1, NN, relay, 0)

    w_up, w_down = (w + 1) % NW, (w + NW - 1) % NW
    n_up, n_down = (n + 1) % NN, (n + NN - 1) % NN

    def halo(slot, src, at, dst):
        moves = (
            (src(3, pl.ds(at, 128)), dst(0, pl.ds(8, 128)), (w_up, n)),
            (src(0, pl.ds(at, 128)), dst(5, pl.ds(8, 128)), (w_down, n)),
            (src(pl.ds(0, 4), pl.ds(at + 120, 8)), dst(pl.ds(1, 4), pl.ds(0, 8)), (w, n_up)),
            (src(pl.ds(0, 4), pl.ds(at, 8)), dst(pl.ds(1, 4), pl.ds(136, 8)), (w, n_down)),
        )
        copies = []
        for i, (a, b, to) in enumerate(moves):
            copies.append(
                pltpu.make_async_remote_copy(
                    src_ref=a,
                    dst_ref=b,
                    send_sem=sem_hs.at[slot, i],
                    recv_sem=sem_hr.at[slot, i],
                    device_id=to,
                    device_id_type=MESH,
                )
            )
        return copies

    head = halo(0, lambda z, y: temp_ref.at[z, y], 0, lambda z, y: tpad.at[z, y])
    head += halo(1, lambda z, y: phase_ref.at[z, y], 0, lambda z, y: ppad.at[z, y])
    for copy in head:
        copy.start()
    lane = lax.broadcasted_iota(jnp.int32, (8, NX), 1)
    own_k = lax.broadcasted_iota(jnp.int32, (8, NX), 0) % 4 + 4 * me
    ex = jnp.sum(jnp.where(lane == own_k, ex_ref[...], 0.0), axis=1, keepdims=True)
    den = ez_ref[...] + ex[None] + ey_ref[...][None]
    inv_ref[...] = (1.0 / den).reshape(ROWS, NX)
    c_ref[...] = jnp.zeros_like(c_ref)
    d_ref[...] = jnp.zeros_like(d_ref)
    press_ref[...] = jnp.zeros_like(press_ref)
    for load in loads:
        load.wait()

    row8 = lax.broadcasted_iota(jnp.int32, (8, NX), 0)
    lane8 = lax.broadcasted_iota(jnp.int32, (8, NX), 1)

    def around(pad, z, i):
        mid = pl.ds(pl.multiple_of(8 + 8 * i, 8), 8)
        low = pl.ds(pl.multiple_of(8 * i, 8), 8)
        high = pl.ds(pl.multiple_of(16 + 8 * i, 8), 8)
        c = pad[z + 1, mid, :]
        up = pad[z + 1, high, :]
        down = pad[z + 1, low, :]
        near = (
            pad[z + 2, mid, :],
            pad[z, mid, :],
            pltpu.roll(jnp.where(row8 == 0, up, c), 7, 0),
            pltpu.roll(jnp.where(row8 == 7, down, c), 1, 0),
            pltpu.roll(c, NX - 1, 1),
            pltpu.roll(c, 1, 1),
        )
        return c, near

    def sweep(copies, body, carry):
        carry = lax.fori_loop(0, 28, lambda q, c: body(1 + q // 14, 1 + q % 14, c), carry, unroll=4)
        copies[2].wait()
        copies[3].wait()
        carry = lax.fori_loop(0, 4, lambda q, c: body(1 + q // 2, 15 * (q % 2), c), carry)
        copies[0].wait()
        copies[1].wait()
        return lax.fori_loop(0, 32, lambda q, c: body(3 * (q // 16), q % 16, c), carry, unroll=4)

    class Both:
        def __init__(self, a, b):
            self.pair = (a, b)

        def wait(self):
            for copy in self.pair:
                copy.wait()

    def head_chunk(z, i, carry):
        rows = pl.ds(pl.multiple_of(8 * (16 * z + i), 8), 8)
        c, near = around(tpad, z, i)
        pc, pnear = around(ppad, z, i)
        gz = jnp.zeros_like(row8) + (4 * w + z)
        gy = row8 + (n * 128 + 8 * i)
        inside = (gz < NZ - 1, gz > 0, gy < NY - 1, gy > 0, lane8 < NX - 1, lane8 > 0)
        conduct = jnp.where(pc > 0, 1.0, 0.4)
        beta = jnp.where(pc > 0, 1.0, 4.0)
        flux = jnp.zeros_like(c)
        faces = jnp.zeros_like(c)
        for q in range(6):
            ins = jnp.where(inside[q], 1.0, 0.0)
            differ = pnear[q] != pc
            flux = flux + ins * jnp.where(differ, -2.0 * c, near[q] - c)
            faces = faces + ins * jnp.where(differ, 1.0, 0.0)
            wts[q, rows, :] = ins * (0.5 * (beta + jnp.where(pnear[q] > 0, 1.0, 4.0)) - 1.0)
        heated = c + 0.06 * conduct * flux
        tnext_ref[z, pl.ds(pl.multiple_of(8 * i, 8), 8), :] = heated
        mass[rows, :] = 2.0 * conduct * faces * heated
        return carry

    sweep([Both(head[i], head[4 + i]) for i in range(4)], head_chunk, 0)
    pl.semaphore_wait(sem_ready, NN - 1)

    ra = lax.broadcasted_iota(jnp.int32, (128, 16), 0)
    ca = lax.broadcasted_iota(jnp.int32, (128, 16), 1)
    pick = jnp.where(ra % 16 == ca, 1.0, 0.0).astype(F32)
    rb = lax.broadcasted_iota(jnp.int32, (128, 128), 0)
    cb = lax.broadcasted_iota(jnp.int32, (128, 128), 1)
    hp = lax.Precision.HIGHEST
    spread = lax.dot_general(pick, north_ref[...], (((1,), (0,)), ((), ())), precision=hp, preferred_element_type=F32)
    spread = lax.dot_general(spread, pick, (((1,), (1,)), ((), ())), precision=hp, preferred_element_type=F32)
    north_all = jnp.where(rb // 16 == cb // 16, spread, 0.0)
    east = east_ref[...]
    for t in range(4):
        lanes = slice(t * 128, (t + 1) * 128)
        across = lax.dot_general(mass[:, lanes], east, (((1,), (1,)), ((), ())), precision=hp, preferred_element_type=F32)
        tile = (rb // 16) * 4 + t
        listed = jnp.zeros((128, 128), F32)
        for e in range(16):
            listed = jnp.where(tile == table_ref[e], 0.3, listed)
        for z in range(4):
            src = lax.dot_general(
                north_all, across[z * 128 : (z + 1) * 128], (((1,), (0,)), ((), ())), precision=hp, preferred_element_type=F32
            )
            f_ref[z * 128 : (z + 1) * 128, lanes] = listed * src
    for z in range(4):
        resid_ref[z] = f_ref[z * 128 : (z + 1) * 128, :]

    half = lax.broadcasted_iota(jnp.int32, (64, 8, 128), 1) < 4
    nn, nt = ((1,), (0,)), ((1,), (1,))

    def parts_of(ref):
        return ref[0], ref[1]

    def bulk(j, src_of, recv, ssem, rsem):
        def send(pw, pn):
            pltpu.make_async_remote_copy(
                src_ref=src_of(pn * NW + pw),
                dst_ref=recv.at[j, me, pl.ds(0, LINES)],
                send_sem=ssem.at[j],
                recv_sem=rsem.at[j],
                device_id=(pw, pn),
                device_id_type=MESH,
            ).start()

        each_peer(w, n, send)

    def wait_others(j, ref, sem):
        part = ref.at[j, pl.ds(0, ND - 1), pl.ds(0, LINES)]
        pltpu.make_async_copy(part, part, sem.at[j]).wait()

    def wait_all(j, ref, sem):
        part = ref.at[j, :, pl.ds(0, LINES)]
        pltpu.make_async_copy(part, part, sem.at[j]).wait()

    def mirrored(piece):
        piece = pltpu.roll(piece, 4, 1)
        return jnp.concatenate([piece[i : i + 1] for i in range(NW - 1, -1, -1)], axis=0)

    def folded(line):
        return line[:, 0:128] + line[:, 128:256] + line[:, 256:384] + line[:, 384:512]

    def summed(rows):
        return jnp.sum(rows, axis=1, keepdims=True)

    def one_pass(j, carry):
        rho, line = carry
        first = j == 0
        table = parts_of(tx_ref)
        low = product(table, split(f_ref[0:256, :]), nt)
        high = product(table, split(f_ref[256:512, :]), nt)
        for zl in range(2):
            a = low[:, zl * 128 : (zl + 1) * 128].reshape(64, 8, 128)
            b = high[:, zl * 128 : (zl + 1) * 128].reshape(64, 8, 128)
            sbf[:, 0, zl * 8 : (zl + 1) * 8, :] = jnp.where(half, a, pltpu.roll(b, 4, 1))
            sbf[:, 1, zl * 8 : (zl + 1) * 8, :] = jnp.where(half, pltpu.roll(a, 4, 1), b)
        sbf[:, :, 16:17, :] = jnp.broadcast_to(line, (64, 2, 1, 128))
        sent = pl.ds(0, LINES)
        own = pltpu.make_async_copy(sbf.at[me // 2, me % 2, sent], recvf.at[j, me, sent], sem_fr.at[j])
        own.start()
        bulk(j, lambda p: sbf.at[p // 2, p % 2, sent], recvf, sem_fs, sem_fr)
        wait_all(j, recvf, sem_fr)
        table = parts_of(ty_ref)
        u = []
        for zl in range(2):
            a = []
            for q in range(NN):
                piece = recvf[j, q * 32 : (q + 1) * 32, zl * 8 : (zl + 1) * 8, :]
                if zl == 1:
                    piece = mirrored(piece)
                a.append(piece.reshape(256, 128))
            u.append(product(split(jnp.concatenate(a, axis=1)), table, nt))
        v = jnp.concatenate(
            [
                product((b_ref[0, 0], b_ref[1, 0]), split(u[0] + u[1]), nn),
                product((b_ref[0, 1], b_ref[1, 1]), split(u[0] - u[1]), nn),
            ],
            axis=0,
        )
        pi = summed(jnp.sum(recvf[j, :, 16:17, :], axis=0))
        alpha = jnp.where(first, -1.0, rho / pi)
        step = jnp.where(first, 0.0, rho / pi)
        left = c_ref[...] - alpha * v
        c_ref[...] = left
        scaled = left * inv_ref[...]
        q_part = jnp.sum(left * scaled, axis=0, keepdims=True)
        sbi[:, 16:17, :] = jnp.broadcast_to(folded(q_part), (ND, 1, 128))
        even = product((bt_ref[0, 0], bt_ref[1, 0]), split(scaled[0:256]), nn)
        odd = product((bt_ref[0, 1], bt_ref[1, 1]), split(scaled[256:512]), nn)
        table = parts_of(ty_ref)
        for zl in range(2):
            r = product(split(even - odd if zl == 1 else even + odd), table, nn)
            for q in range(NN):
                piece = r[:, q * 128 : (q + 1) * 128].reshape(32, 8, 128)
                if zl == 1:
                    piece = mirrored(piece)
                sbi[q * 32 : (q + 1) * 32, zl * 8 : (zl + 1) * 8, :] = piece
        own = pltpu.make_async_copy(sbi.at[me, sent], recvi.at[j, me, sent], sem_ir.at[j])
        own.start()
        bulk(j, lambda p: sbi.at[p, sent], recvi, sem_is, sem_ir)

        def update(g, carry):
            z, i = g // 16, g % 16
            rows = pl.ds(pl.multiple_of(8 * g, 8), 8)
            line = pl.ds(pl.multiple_of(8 * i, 8), 8)
            press_ref[z, line, :] = press_ref[z, line, :] + step * d_ref[rows, :]
            resid_ref[z, line, :] = resid_ref[z, line, :] - step * f_ref[rows, :]
            return carry

        lax.fori_loop(0, 64, update, 0, unroll=4)
        wait_others(j, recvf, sem_fs)
        wait_all(j, recvi, sem_ir)
        wait_others(j, recvi, sem_is)
        def layer(z):
            zl = z % 2
            got = recvi[j, :, zl * 8 : (zl + 1) * 8, :].reshape(64, 2, 8, 128)
            even, odd = got[:, 0], got[:, 1]
            if z < 2:
                rows = jnp.where(half, even, pltpu.roll(odd, 4, 1))
            else:
                rows = jnp.where(half, pltpu.roll(even, 4, 1), odd)
            return rows.reshape(ROWS, 128).T

        table = parts_of(tx_ref)
        field = spad.at[j]
        copies = halo(2 + j, lambda z, y: field.at[(z + 1) if isinstance(z, int) else pl.ds(1, 4), y], 8, lambda z, y: field.at[z, y])
        for z in ((0, 3), (1, 2)):
            r = product(split(jnp.concatenate([layer(q) for q in z], axis=0)), table, nn)
            spad[j, 1 + z[0], 8:136, :] = r[0:128]
            spad[j, 1 + z[1], 8:136, :] = r[128:256]
            if z[0] == 0:
                copies[0].start()
                copies[1].start()
        copies[2].start()
        copies[3].start()
        fresh = summed(jnp.sum(recvi[j, :, 16:17, :], axis=0))
        mix = jnp.where(first, 0.0, fresh / rho)

        def stencil(z, i, carry):
            rows = pl.ds(pl.multiple_of(8 * (16 * z + i), 8), 8)
            c, near = around(field, z, i)
            total = resid_ref[z, pl.ds(pl.multiple_of(8 * i, 8), 8), :] + mix * f_ref[rows, :]
            for q in range(6):
                total = total + wts[q, rows, :] * (c - near[q])
            f_ref[rows, :] = total
            d = c + mix * d_ref[rows, :]
            d_ref[rows, :] = d
            return carry + d * total

        line = jnp.sum(sweep(copies, stencil, jnp.zeros((8, NX), F32)), axis=0, keepdims=True)
        return fresh, folded(line)

    rho, line = lax.fori_loop(0, ITERS, one_pass, (jnp.ones((1, 1), F32), jnp.ones((1, 128), F32)))

    def gather(slots, slot, count, to, ssem, rsem):
        def send(step, carry):
            pltpu.make_async_remote_copy(
                src_ref=slots.at[slot],
                dst_ref=slots.at[slot],
                send_sem=ssem,
                recv_sem=rsem,
                device_id=to(step),
                device_id_type=MESH,
            ).start()
            return carry

        lax.fori_loop(1, count, send, 0)
        part = slots.at[pl.ds(0, count - 1)]
        pltpu.make_async_copy(part, part, rsem).wait()
        pltpu.make_async_copy(part, part, ssem).wait()
        return jnp.sum(slots[...], axis=0)

    red_n[n] = line
    red_w[w] = gather(red_n, n, NN, lambda step: (w, (n + step) % NN), sem_rs.at[0], sem_rr.at[0])
    pi = summed(gather(red_w, w, NW, lambda step: ((w + step) % NW, n), sem_rs.at[1], sem_rr.at[1]))
    alpha = rho / pi

    def finish(g, carry):
        z, i = g // 16, g % 16
        rows = pl.ds(pl.multiple_of(8 * g, 8), 8)
        line = pl.ds(pl.multiple_of(8 * i, 8), 8)
        press_ref[z, line, :] = press_ref[z, line, :] + alpha * d_ref[rows, :]
        resid_ref[z, line, :] = resid_ref[z, line, :] - alpha * f_ref[rows, :]
        return carry

    lax.fori_loop(0, 64, finish, 0, unroll=4)


def hand_on(a, b, c, d, e, f):
    d[...] = a[...]
    e[...] = b[...]
    f[...] = c[...]


def on_device(temp, phase, table, north, east):
    ez = np.concatenate([eigen_np(NZ)[0::2], eigen_np(NZ)[1::2]]) + 0.01
    ez = np.repeat(ez, 4).reshape(64, 8, 1).astype(np.float32)
    ey = eigen_np(NY).astype(np.float32).reshape(1, NY)
    ex = eigen_np(NX).astype(np.float32).reshape(1, NX)
    bz = z_table()
    tables = [jnp.asarray(split_np(t)) for t in (cosine_np(NX), cosine_np(NY), bz, bz.transpose(0, 2, 1))]
    vmem = pl.BlockSpec(memory_space=pltpu.VMEM)
    anywhere = pl.BlockSpec(memory_space=pl.ANY)
    tabled = pltpu.VMEM((2, ROWS, ROWS), BF16)
    folded = pltpu.VMEM((2, 2, 256, 256), BF16)
    smem = pl.BlockSpec(memory_space=pltpu.SMEM)
    shape = jax.ShapeDtypeStruct((4, 128, NX), F32)
    dma = pltpu.SemaphoreType.DMA
    square = pltpu.VMEM((ROWS, NX), F32)
    results = pl.pallas_call(
        whole_kernel,
        out_shape=(shape, shape, shape),
        in_specs=[anywhere, anywhere, smem, vmem, vmem] + [anywhere] * 4 + [vmem] * 3,
        out_specs=(vmem, vmem, vmem),
        scratch_shapes=[
            tabled,
            tabled,
            folded,
            folded,
            pltpu.VMEM((6, 144, NX), F32),
            pltpu.VMEM((6, 144, NX), jnp.int32),
            pltpu.VMEM((ITERS, 6, 144, NX), F32),
            pltpu.VMEM((6, ROWS, NX), F32),
            square,
            square,
            square,
            square,
            square,
            pltpu.VMEM((64, 2, 24, 128), F32),
            pltpu.VMEM((ND, 24, 128), F32),
            pltpu.VMEM((ITERS, ND, 24, 128), F32),
            pltpu.VMEM((ITERS, ND, 24, 128), F32),
            pltpu.VMEM((NN, 1, 128), F32),
            pltpu.VMEM((NW, 1, 128), F32),
            dma((ITERS,)),
            dma((ITERS,)),
            dma((ITERS,)),
            dma((ITERS,)),
            dma((2,)),
            dma((2,)),
            dma((5, 4)),
            dma((5, 4)),
            pltpu.SemaphoreType.REGULAR,
            dma((6,)),
        ],
        compiler_params=pltpu.CompilerParams(
            collective_id=0, has_side_effects=True, vmem_limit_bytes=60 * 2**20
        ),
    )(temp, phase, table.reshape(16), north, east, *tables, jnp.asarray(ez), jnp.asarray(ey), jnp.asarray(ex))
    layer = pl.BlockSpec((1, 128, NX), lambda z: (z, 0, 0))
    return pl.pallas_call(
        hand_on,
        grid=(4,),
        out_shape=(shape, shape, shape),
        in_specs=[layer] * 3,
        out_specs=(layer, layer, layer),
    )(*results)


def solution(mesh):
    block = P("wide", "narrow", None)
    return jax.shard_map(
        on_device,
        mesh=mesh,
        in_specs=(block, block, block, P(), P()),
        out_specs=(block, block, block),
        check_vma=False,
    )
```

```python
import functools
import math

import jax
import jax.numpy as jnp
import ml_dtypes
import numpy as np
from jax import lax
from jax.experimental import pallas as pl
from jax.experimental.pallas import tpu as pltpu
from jax.sharding import PartitionSpec as P

MESH = pl.DeviceIdType.MESH
F32 = jnp.float32
BF16 = jnp.bfloat16
NX, NY, NZ = 512, 512, 128
NW, NN = 32, 4
ND = NW * NN
ITERS = 3
ROWS = 512
LINES = 17


def cosine_np(m):
    k = np.arange(m)[:, None]
    i = np.arange(m)[None, :]
    scale = np.where(k == 0, math.sqrt(1.0 / m), math.sqrt(2.0 / m))
    return scale * np.cos(np.pi * ((k * (2 * i + 1)) % (4 * m)) / (2 * m))


def eigen_np(m):
    return 4.0 * np.sin(np.pi * np.arange(m) / (2 * m)) ** 2


def split_np(table):
    parts = []
    rest = table.astype(np.float64)
    for _ in range(2):
        part = rest.astype(np.float32).astype(ml_dtypes.bfloat16)
        parts.append(part)
        rest = rest - part.astype(np.float64)
    return np.stack(parts)


def z_table():
    table = cosine_np(NZ)[:, 0::2].reshape(NZ // 2, 2, NZ // 2)
    big = np.zeros((2, NZ // 2, 4, NZ // 2, 4))
    for k in range(4):
        big[:, :, k, :, k] = table.transpose(1, 0, 2)
    return big.reshape(2, 256, 256)


def split(x):
    high = x.astype(BF16)
    return high, (x - high.astype(F32)).astype(BF16)


def product(a, b, dims):
    total = None
    for i, j in ((0, 1), (1, 0), (0, 0)):
        term = lax.dot_general(a[i], b[j], (dims, ((), ())), preferred_element_type=F32)
        total = term if total is None else total + term
    return total


HOPS = sorted(np.ndindex(3, 3, 3), key=lambda hops: -sum(hops))


def each_peer(w, n, send):
    y, z, c = w // 8, (w // 2) % 4, w % 2
    for hops in HOPS:
        ones = sum(h == 1 for h in hops)

        def body(turn, carry, hops=hops):
            flip, rest = turn % 2, turn // 2
            offset = []
            for h in hops:
                if h == 1:
                    offset.append(1 + 2 * (rest % 2))
                    rest = rest // 2
                else:
                    offset.append(h)
            dx, dy, dz = offset
            send(((y + dy) % 4) * 8 + ((z + dz) % 4) * 2 + (c + flip) % 2, (n + dx) % 4)
            return carry

        lax.fori_loop(1 if sum(hops) == 0 else 0, 2 ** (ones + 1), body, 0)


def whole_kernel(
    temp_ref, phase_ref, table_ref, north_ref, east_ref, tx_any, ty_any, b_any, bt_any, ez_ref, ey_ref, ex_ref,
    tnext_any, press_any, resid_any,
    tnext_ref, press_ref, resid_ref,
    tx_ref, ty_ref, b_ref, bt_ref, tpad, ppad, spad, wts, mass, f_ref, c_ref, d_ref, inv_ref,
    sbf, sbi, recvf, recvi, red_n, red_w,
    sem_fs, sem_fr, sem_is, sem_ir, sem_rs, sem_rr, sem_hs, sem_hr, sem_ready, sem_load, sem_store,
):
    w = lax.axis_index("wide")
    n = lax.axis_index("narrow")
    me = n * NW + w

    barrier = pltpu.get_barrier_semaphore()
    loads = [
        pltpu.make_async_copy(a, b, sem_load.at[i])
        for i, (a, b) in enumerate(
            (
                (temp_ref, tpad.at[pl.ds(1, 4), pl.ds(8, 128)]),
                (phase_ref, ppad.at[pl.ds(1, 4), pl.ds(8, 128)]),
                (tx_any, tx_ref),
                (ty_any, ty_ref),
                (b_any, b_ref),
                (bt_any, bt_ref),
            )
        )
    ]
    for load in loads:
        load.start()

    def greet_narrow(step, carry):
        pl.semaphore_signal(barrier, inc=1, device_id=(w, (n + step) % NN), device_id_type=MESH)
        return carry

    def greet_wide(step, carry):
        pl.semaphore_signal(barrier, inc=1, device_id=((w + step) % NW, n), device_id_type=MESH)
        return carry

    lax.fori_loop(1, NN, greet_narrow, 0)
    lax.fori_loop(1, NW, greet_wide, 0)

    pl.semaphore_wait(barrier, NN - 1 + NW - 1)

    def relay(step, carry):
        pl.semaphore_signal(sem_ready, inc=1, device_id=(w, (n + step) % NN), device_id_type=MESH)
        return carry

    lax.fori_loop(1, NN, relay, 0)

    w_up, w_down = (w + 1) % NW, (w + NW - 1) % NW
    n_up, n_down = (n + 1) % NN, (n + NN - 1) % NN

    def halo(slot, src, at, dst):
        moves = (
            (src(3, pl.ds(at, 128)), dst(0, pl.ds(8, 128)), (w_up, n)),
            (src(0, pl.ds(at, 128)), dst(5, pl.ds(8, 128)), (w_down, n)),
            (src(pl.ds(0, 4), pl.ds(at + 120, 8)), dst(pl.ds(1, 4), pl.ds(0, 8)), (w, n_up)),
            (src(pl.ds(0, 4), pl.ds(at, 8)), dst(pl.ds(1, 4), pl.ds(136, 8)), (w, n_down)),
        )
        copies = []
        for i, (a, b, to) in enumerate(moves):
            copies.append(
                pltpu.make_async_remote_copy(
                    src_ref=a,
                    dst_ref=b,
                    send_sem=sem_hs.at[slot, i],
                    recv_sem=sem_hr.at[slot, i],
                    device_id=to,
                    device_id_type=MESH,
                )
            )
        return copies

    head = halo(0, lambda z, y: temp_ref.at[z, y], 0, lambda z, y: tpad.at[z, y])
    head += halo(1, lambda z, y: phase_ref.at[z, y], 0, lambda z, y: ppad.at[z, y])
    for copy in head:
        copy.start()
    lane = lax.broadcasted_iota(jnp.int32, (8, NX), 1)
    own_k = lax.broadcasted_iota(jnp.int32, (8, NX), 0) % 4 + 4 * me
    ex = jnp.sum(jnp.where(lane == own_k, ex_ref[...], 0.0), axis=1, keepdims=True)
    den = ez_ref[...] + ex[None] + ey_ref[...][None]
    inv_ref[...] = (1.0 / den).reshape(ROWS, NX)
    c_ref[...] = jnp.zeros_like(c_ref)
    d_ref[...] = jnp.zeros_like(d_ref)
    press_ref[...] = jnp.zeros_like(press_ref)
    for load in loads:
        load.wait()

    row8 = lax.broadcasted_iota(jnp.int32, (8, NX), 0)
    lane8 = lax.broadcasted_iota(jnp.int32, (8, NX), 1)

    def around(pad, z, i):
        mid = pl.ds(pl.multiple_of(8 + 8 * i, 8), 8)
        low = pl.ds(pl.multiple_of(8 * i, 8), 8)
        high = pl.ds(pl.multiple_of(16 + 8 * i, 8), 8)
        c = pad[z + 1, mid, :]
        up = pad[z + 1, high, :]
        down = pad[z + 1, low, :]
        near = (
            pad[z + 2, mid, :],
            pad[z, mid, :],
            pltpu.roll(jnp.where(row8 == 0, up, c), 7, 0),
            pltpu.roll(jnp.where(row8 == 7, down, c), 1, 0),
            pltpu.roll(c, NX - 1, 1),
            pltpu.roll(c, 1, 1),
        )
        return c, near

    def sweep(copies, body, carry):
        carry = lax.fori_loop(0, 28, lambda q, c: body(1 + q // 14, 1 + q % 14, c), carry, unroll=4)
        copies[2].wait()
        copies[3].wait()
        carry = lax.fori_loop(0, 4, lambda q, c: body(1 + q // 2, 15 * (q % 2), c), carry)
        copies[0].wait()
        copies[1].wait()
        return lax.fori_loop(0, 32, lambda q, c: body(3 * (q // 16), q % 16, c), carry, unroll=4)

    class Both:
        def __init__(self, a, b):
            self.pair = (a, b)

        def wait(self):
            for copy in self.pair:
                copy.wait()

    def head_chunk(z, i, carry):
        rows = pl.ds(pl.multiple_of(8 * (16 * z + i), 8), 8)
        c, near = around(tpad, z, i)
        pc, pnear = around(ppad, z, i)
        gz = jnp.zeros_like(row8) + (4 * w + z)
        gy = row8 + (n * 128 + 8 * i)
        inside = (gz < NZ - 1, gz > 0, gy < NY - 1, gy > 0, lane8 < NX - 1, lane8 > 0)
        conduct = jnp.where(pc > 0, 1.0, 0.4)
        beta = jnp.where(pc > 0, 1.0, 4.0)
        flux = jnp.zeros_like(c)
        faces = jnp.zeros_like(c)
        for q in range(6):
            ins = jnp.where(inside[q], 1.0, 0.0)
            differ = pnear[q] != pc
            flux = flux + ins * jnp.where(differ, -2.0 * c, near[q] - c)
            faces = faces + ins * jnp.where(differ, 1.0, 0.0)
            wts[q, rows, :] = ins * (0.5 * (beta + jnp.where(pnear[q] > 0, 1.0, 4.0)) - 1.0)
        heated = c + 0.06 * conduct * flux
        tnext_ref[z, pl.ds(pl.multiple_of(8 * i, 8), 8), :] = heated
        mass[rows, :] = 2.0 * conduct * faces * heated
        return carry

    sweep([Both(head[i], head[4 + i]) for i in range(4)], head_chunk, 0)
    stores = [pltpu.make_async_copy(tnext_ref, tnext_any, sem_store.at[8])]
    stores[0].start()
    pl.semaphore_wait(sem_ready, NN - 1)

    ra = lax.broadcasted_iota(jnp.int32, (128, 16), 0)
    ca = lax.broadcasted_iota(jnp.int32, (128, 16), 1)
    pick = jnp.where(ra % 16 == ca, 1.0, 0.0).astype(F32)
    rb = lax.broadcasted_iota(jnp.int32, (128, 128), 0)
    cb = lax.broadcasted_iota(jnp.int32, (128, 128), 1)
    hp = lax.Precision.HIGHEST
    spread = lax.dot_general(pick, north_ref[...], (((1,), (0,)), ((), ())), precision=hp, preferred_element_type=F32)
    spread = lax.dot_general(spread, pick, (((1,), (1,)), ((), ())), precision=hp, preferred_element_type=F32)
    north_all = jnp.where(rb // 16 == cb // 16, spread, 0.0)
    east = east_ref[...]
    for t in range(4):
        lanes = slice(t * 128, (t + 1) * 128)
        across = lax.dot_general(mass[:, lanes], east, (((1,), (1,)), ((), ())), precision=hp, preferred_element_type=F32)
        tile = (rb // 16) * 4 + t
        listed = jnp.zeros((128, 128), F32)
        for e in range(16):
            listed = jnp.where(tile == table_ref[e], 0.3, listed)
        for z in range(4):
            src = lax.dot_general(
                north_all, across[z * 128 : (z + 1) * 128], (((1,), (0,)), ((), ())), precision=hp, preferred_element_type=F32
            )
            f_ref[z * 128 : (z + 1) * 128, lanes] = listed * src
    for z in range(4):
        resid_ref[z] = f_ref[z * 128 : (z + 1) * 128, :]

    half = lax.broadcasted_iota(jnp.int32, (64, 8, 128), 1) < 4
    nn, nt = ((1,), (0,)), ((1,), (1,))

    def parts_of(ref):
        return ref[0], ref[1]

    def bulk(j, src_of, recv, ssem, rsem):
        def send(pw, pn):
            pltpu.make_async_remote_copy(
                src_ref=src_of(pn * NW + pw),
                dst_ref=recv.at[j, me, pl.ds(0, LINES)],
                send_sem=ssem.at[j],
                recv_sem=rsem.at[j],
                device_id=(pw, pn),
                device_id_type=MESH,
            ).start()

        each_peer(w, n, send)

    def wait_others(j, ref, sem):
        part = ref.at[j, pl.ds(0, ND - 1), pl.ds(0, LINES)]
        pltpu.make_async_copy(part, part, sem.at[j]).wait()

    def wait_all(j, ref, sem):
        part = ref.at[j, :, pl.ds(0, LINES)]
        pltpu.make_async_copy(part, part, sem.at[j]).wait()

    def mirrored(piece):
        piece = pltpu.roll(piece, 4, 1)
        return jnp.concatenate([piece[i : i + 1] for i in range(NW - 1, -1, -1)], axis=0)

    def folded(line):
        return line[:, 0:128] + line[:, 128:256] + line[:, 256:384] + line[:, 384:512]

    def summed(rows):
        return jnp.sum(rows, axis=1, keepdims=True)

    def one_pass(j, carry):
        rho, line = carry
        first = j == 0
        table = parts_of(tx_ref)
        low = product(table, split(f_ref[0:256, :]), nt)
        high = product(table, split(f_ref[256:512, :]), nt)
        for zl in range(2):
            a = low[:, zl * 128 : (zl + 1) * 128].reshape(64, 8, 128)
            b = high[:, zl * 128 : (zl + 1) * 128].reshape(64, 8, 128)
            sbf[:, 0, zl * 8 : (zl + 1) * 8, :] = jnp.where(half, a, pltpu.roll(b, 4, 1))
            sbf[:, 1, zl * 8 : (zl + 1) * 8, :] = jnp.where(half, pltpu.roll(a, 4, 1), b)
        sbf[:, :, 16:17, :] = jnp.broadcast_to(line, (64, 2, 1, 128))
        sent = pl.ds(0, LINES)
        own = pltpu.make_async_copy(sbf.at[me // 2, me % 2, sent], recvf.at[j, me, sent], sem_fr.at[j])
        own.start()
        bulk(j, lambda p: sbf.at[p // 2, p % 2, sent], recvf, sem_fs, sem_fr)
        wait_all(j, recvf, sem_fr)
        table = parts_of(ty_ref)
        u = []
        for zl in range(2):
            a = []
            for q in range(NN):
                piece = recvf[j, q * 32 : (q + 1) * 32, zl * 8 : (zl + 1) * 8, :]
                if zl == 1:
                    piece = mirrored(piece)
                a.append(piece.reshape(256, 128))
            u.append(product(split(jnp.concatenate(a, axis=1)), table, nt))
        v = jnp.concatenate(
            [
                product((b_ref[0, 0], b_ref[1, 0]), split(u[0] + u[1]), nn),
                product((b_ref[0, 1], b_ref[1, 1]), split(u[0] - u[1]), nn),
            ],
            axis=0,
        )
        pi = summed(jnp.sum(recvf[j, :, 16:17, :], axis=0))
        alpha = jnp.where(first, -1.0, rho / pi)
        step = jnp.where(first, 0.0, rho / pi)
        left = c_ref[...] - alpha * v
        c_ref[...] = left
        scaled = left * inv_ref[...]
        q_part = jnp.sum(left * scaled, axis=0, keepdims=True)
        sbi[:, 16:17, :] = jnp.broadcast_to(folded(q_part), (ND, 1, 128))
        even = product((bt_ref[0, 0], bt_ref[1, 0]), split(scaled[0:256]), nn)
        odd = product((bt_ref[0, 1], bt_ref[1, 1]), split(scaled[256:512]), nn)
        table = parts_of(ty_ref)
        for zl in range(2):
            r = product(split(even - odd if zl == 1 else even + odd), table, nn)
            for q in range(NN):
                piece = r[:, q * 128 : (q + 1) * 128].reshape(32, 8, 128)
                if zl == 1:
                    piece = mirrored(piece)
                sbi[q * 32 : (q + 1) * 32, zl * 8 : (zl + 1) * 8, :] = piece
        own = pltpu.make_async_copy(sbi.at[me, sent], recvi.at[j, me, sent], sem_ir.at[j])
        own.start()
        bulk(j, lambda p: sbi.at[p, sent], recvi, sem_is, sem_ir)

        def update(g, carry):
            z, i = g // 16, g % 16
            rows = pl.ds(pl.multiple_of(8 * g, 8), 8)
            line = pl.ds(pl.multiple_of(8 * i, 8), 8)
            press_ref[z, line, :] = press_ref[z, line, :] + step * d_ref[rows, :]
            resid_ref[z, line, :] = resid_ref[z, line, :] - step * f_ref[rows, :]
            return carry

        lax.fori_loop(0, 64, update, 0, unroll=4)
        wait_others(j, recvf, sem_fs)
        wait_all(j, recvi, sem_ir)
        wait_others(j, recvi, sem_is)
        def layer(z):
            zl = z % 2
            got = recvi[j, :, zl * 8 : (zl + 1) * 8, :].reshape(64, 2, 8, 128)
            even, odd = got[:, 0], got[:, 1]
            if z < 2:
                rows = jnp.where(half, even, pltpu.roll(odd, 4, 1))
            else:
                rows = jnp.where(half, pltpu.roll(even, 4, 1), odd)
            return rows.reshape(ROWS, 128).T

        table = parts_of(tx_ref)
        field = spad.at[j]
        copies = halo(2 + j, lambda z, y: field.at[(z + 1) if isinstance(z, int) else pl.ds(1, 4), y], 8, lambda z, y: field.at[z, y])
        for z in ((0, 3), (1, 2)):
            r = product(split(jnp.concatenate([layer(q) for q in z], axis=0)), table, nn)
            spad[j, 1 + z[0], 8:136, :] = r[0:128]
            spad[j, 1 + z[1], 8:136, :] = r[128:256]
            if z[0] == 0:
                copies[0].start()
                copies[1].start()
        copies[2].start()
        copies[3].start()
        fresh = summed(jnp.sum(recvi[j, :, 16:17, :], axis=0))
        mix = jnp.where(first, 0.0, fresh / rho)

        def stencil(z, i, carry):
            rows = pl.ds(pl.multiple_of(8 * (16 * z + i), 8), 8)
            c, near = around(field, z, i)
            total = resid_ref[z, pl.ds(pl.multiple_of(8 * i, 8), 8), :] + mix * f_ref[rows, :]
            for q in range(6):
                total = total + wts[q, rows, :] * (c - near[q])
            f_ref[rows, :] = total
            d = c + mix * d_ref[rows, :]
            d_ref[rows, :] = d
            return carry + d * total

        line = jnp.sum(sweep(copies, stencil, jnp.zeros((8, NX), F32)), axis=0, keepdims=True)
        return fresh, folded(line)

    rho, line = lax.fori_loop(0, ITERS, one_pass, (jnp.ones((1, 1), F32), jnp.ones((1, 128), F32)))

    def gather(slots, slot, count, to, ssem, rsem):
        def send(step, carry):
            pltpu.make_async_remote_copy(
                src_ref=slots.at[slot],
                dst_ref=slots.at[slot],
                send_sem=ssem,
                recv_sem=rsem,
                device_id=to(step),
                device_id_type=MESH,
            ).start()
            return carry

        lax.fori_loop(1, count, send, 0)
        part = slots.at[pl.ds(0, count - 1)]
        pltpu.make_async_copy(part, part, rsem).wait()
        pltpu.make_async_copy(part, part, ssem).wait()
        return jnp.sum(slots[...], axis=0)

    y, z, c = w // 8, (w // 2) % 4, w % 2
    mine = n * 2 + c
    red_n[mine] = line
    red_w[w // 2] = gather(
        red_n, mine, 8, lambda t: (w - c + (c + t) % 2, (n + t // 2) % 4), sem_rs.at[0], sem_rr.at[0]
    )
    pi = gather(
        red_w,
        w // 2,
        16,
        lambda t: (((y + t // 4) % 4) * 8 + ((z + t) % 4) * 2 + c, n),
        sem_rs.at[1],
        sem_rr.at[1],
    )
    pi = summed(pi)
    alpha = rho / pi

    for z in range(4):

        def finish(i, carry):
            rows = pl.ds(pl.multiple_of(128 * z + 8 * i, 8), 8)
            line = pl.ds(pl.multiple_of(8 * i, 8), 8)
            press_ref[z, line, :] = press_ref[z, line, :] + alpha * d_ref[rows, :]
            resid_ref[z, line, :] = resid_ref[z, line, :] - alpha * f_ref[rows, :]
            return carry

        lax.fori_loop(0, 16, finish, 0, unroll=4)
        for i, (a, b) in enumerate(((press_ref, press_any), (resid_ref, resid_any))):
            stores.append(pltpu.make_async_copy(a.at[z], b.at[z], sem_store.at[2 * z + i]))
            stores[-1].start()
    for store in stores:
        store.wait()


def hand_on(a, b, c, d, e, f, held, sem_in, sem_out):
    moves = []
    for i, (source, target) in enumerate(((a, d), (b, e), (c, f))):
        for z in (0, 2):
            at = pl.ds(z, 2)
            k = 2 * i + z // 2
            slot = held.at[k]
            moves.append(
                (
                    pltpu.make_async_copy(source.at[at], slot, sem_in.at[k]),
                    pltpu.make_async_copy(slot, target.at[at], sem_out.at[k]),
                )
            )
    for load, _ in moves:
        load.start()
    for load, store in moves:
        load.wait()
        store.start()
    for _, store in moves:
        store.wait()


def on_device(temp, phase, table, north, east):
    ez = np.concatenate([eigen_np(NZ)[0::2], eigen_np(NZ)[1::2]]) + 0.01
    ez = np.repeat(ez, 4).reshape(64, 8, 1).astype(np.float32)
    ey = eigen_np(NY).astype(np.float32).reshape(1, NY)
    ex = eigen_np(NX).astype(np.float32).reshape(1, NX)
    bz = z_table()
    tables = [jnp.asarray(split_np(t)) for t in (cosine_np(NX), cosine_np(NY), bz, bz.transpose(0, 2, 1))]
    vmem = pl.BlockSpec(memory_space=pltpu.VMEM)
    anywhere = pl.BlockSpec(memory_space=pl.ANY)
    tabled = pltpu.VMEM((2, ROWS, ROWS), BF16)
    folded = pltpu.VMEM((2, 2, 256, 256), BF16)
    block = pltpu.VMEM((4, 128, NX), F32)
    smem = pl.BlockSpec(memory_space=pltpu.SMEM)
    shape = jax.ShapeDtypeStruct((4, 128, NX), F32)
    dma = pltpu.SemaphoreType.DMA
    square = pltpu.VMEM((ROWS, NX), F32)
    results = pl.pallas_call(
        whole_kernel,
        out_shape=(shape, shape, shape),
        in_specs=[anywhere, anywhere, smem, vmem, vmem] + [anywhere] * 4 + [vmem] * 3,
        out_specs=(anywhere, anywhere, anywhere),
        scratch_shapes=[
            block,
            block,
            block,
            tabled,
            tabled,
            folded,
            folded,
            pltpu.VMEM((6, 144, NX), F32),
            pltpu.VMEM((6, 144, NX), jnp.int32),
            pltpu.VMEM((ITERS, 6, 144, NX), F32),
            pltpu.VMEM((6, ROWS, NX), F32),
            square,
            square,
            square,
            square,
            square,
            pltpu.VMEM((64, 2, 24, 128), F32),
            pltpu.VMEM((ND, 24, 128), F32),
            pltpu.VMEM((ITERS, ND, 24, 128), F32),
            pltpu.VMEM((ITERS, ND, 24, 128), F32),
            pltpu.VMEM((8, 1, 128), F32),
            pltpu.VMEM((16, 1, 128), F32),
            dma((ITERS,)),
            dma((ITERS,)),
            dma((ITERS,)),
            dma((ITERS,)),
            dma((2,)),
            dma((2,)),
            dma((5, 4)),
            dma((5, 4)),
            pltpu.SemaphoreType.REGULAR,
            dma((6,)),
            dma((9,)),
        ],
        compiler_params=pltpu.CompilerParams(
            collective_id=0, has_side_effects=True, vmem_limit_bytes=60 * 2**20
        ),
    )(temp, phase, table.reshape(16), north, east, *tables, jnp.asarray(ez), jnp.asarray(ey), jnp.asarray(ex))
    return pl.pallas_call(
        hand_on,
        out_shape=(shape, shape, shape),
        in_specs=[anywhere] * 3,
        out_specs=(anywhere, anywhere, anywhere),
        scratch_shapes=[pltpu.VMEM((6, 2, 128, NX), F32), dma((6,)), dma((6,))],
        compiler_params=pltpu.CompilerParams(vmem_limit_bytes=60 * 2**20),
    )(*results)


def solution(mesh):
    block = P("wide", "narrow", None)
    return jax.shard_map(
        on_device,
        mesh=mesh,
        in_specs=(block, block, block, P(), P()),
        out_specs=(block, block, block),
        check_vma=False,
    )
```

```python
import functools
import math

import jax
import jax.numpy as jnp
import ml_dtypes
import numpy as np
from jax import lax
from jax.experimental import pallas as pl
from jax.experimental.pallas import tpu as pltpu
from jax.sharding import PartitionSpec as P

MESH = pl.DeviceIdType.MESH
F32 = jnp.float32
BF16 = jnp.bfloat16
NX, NY, NZ = 512, 512, 128
NW, NN = 32, 4
ND = NW * NN
ITERS = 3
ROWS = 512
LINES = 17


def cosine_np(m):
    k = np.arange(m)[:, None]
    i = np.arange(m)[None, :]
    scale = np.where(k == 0, math.sqrt(1.0 / m), math.sqrt(2.0 / m))
    return scale * np.cos(np.pi * ((k * (2 * i + 1)) % (4 * m)) / (2 * m))


def eigen_np(m):
    return 4.0 * np.sin(np.pi * np.arange(m) / (2 * m)) ** 2


def split_np(table):
    parts = []
    rest = table.astype(np.float64)
    for _ in range(2):
        part = rest.astype(np.float32).astype(ml_dtypes.bfloat16)
        parts.append(part)
        rest = rest - part.astype(np.float64)
    return np.stack(parts)


def z_table():
    table = cosine_np(NZ)[:, 0::2].reshape(NZ // 2, 2, NZ // 2)
    big = np.zeros((2, NZ // 2, 4, NZ // 2, 4))
    for k in range(4):
        big[:, :, k, :, k] = table.transpose(1, 0, 2)
    return big.reshape(2, 256, 256)


def split(x):
    high = x.astype(BF16)
    return high, (x - high.astype(F32)).astype(BF16)


def product(a, b, dims):
    total = None
    for i, j in ((0, 1), (1, 0), (0, 0)):
        term = lax.dot_general(a[i], b[j], (dims, ((), ())), preferred_element_type=F32)
        total = term if total is None else total + term
    return total


HOPS = sorted(np.ndindex(3, 3, 3), key=lambda hops: -sum(hops))


def each_peer(w, n, send):
    y, z, c = w // 8, (w // 2) % 4, w % 2
    for hops in HOPS:
        ones = sum(h == 1 for h in hops)

        def body(turn, carry, hops=hops):
            flip, rest = turn % 2, turn // 2
            offset = []
            for h in hops:
                if h == 1:
                    offset.append(1 + 2 * (rest % 2))
                    rest = rest // 2
                else:
                    offset.append(h)
            dx, dy, dz = offset
            send(((y + dy) % 4) * 8 + ((z + dz) % 4) * 2 + (c + flip) % 2, (n + dx) % 4)
            return carry

        lax.fori_loop(1 if sum(hops) == 0 else 0, 2 ** (ones + 1), body, 0, unroll=min(4, 2**ones))


def whole_kernel(
    temp_ref, phase_ref, table_ref, north_ref, east_ref, tx_any, ty_any, b_any, bt_any, ez_ref, ey_ref, ex_ref,
    tnext_any, press_any, resid_any,
    tnext_ref, press_ref, resid_ref,
    tx_ref, ty_ref, b_ref, bt_ref, tpad, ppad, spad, wts, mass, f_ref, c_ref, d_ref, inv_ref,
    sbf, sbi, recvf, recvi, red_n, red_w,
    sem_fs, sem_fr, sem_is, sem_ir, sem_rs, sem_rr, sem_hs, sem_hr, sem_ready, sem_load, sem_store,
):
    w = lax.axis_index("wide")
    n = lax.axis_index("narrow")
    me = n * NW + w

    barrier = pltpu.get_barrier_semaphore()
    loads = [
        pltpu.make_async_copy(a, b, sem_load.at[i])
        for i, (a, b) in enumerate(
            (
                (temp_ref, tpad.at[pl.ds(1, 4), pl.ds(8, 128)]),
                (phase_ref, ppad.at[pl.ds(1, 4), pl.ds(8, 128)]),
                (tx_any, tx_ref),
                (ty_any, ty_ref),
                (b_any, b_ref),
                (bt_any, bt_ref),
            )
        )
    ]
    for load in loads:
        load.start()

    def greet_narrow(step, carry):
        pl.semaphore_signal(barrier, inc=1, device_id=(w, (n + step) % NN), device_id_type=MESH)
        return carry

    def greet_wide(step, carry):
        pl.semaphore_signal(barrier, inc=1, device_id=((w + step) % NW, n), device_id_type=MESH)
        return carry

    lax.fori_loop(1, NN, greet_narrow, 0)
    lax.fori_loop(1, NW, greet_wide, 0)

    pl.semaphore_wait(barrier, NN - 1 + NW - 1)

    def relay(step, carry):
        pl.semaphore_signal(sem_ready, inc=1, device_id=(w, (n + step) % NN), device_id_type=MESH)
        return carry

    lax.fori_loop(1, NN, relay, 0)

    w_up, w_down = (w + 1) % NW, (w + NW - 1) % NW
    n_up, n_down = (n + 1) % NN, (n + NN - 1) % NN

    def halo(slot, src, at, dst):
        moves = (
            (src(3, pl.ds(at, 128)), dst(0, pl.ds(8, 128)), (w_up, n)),
            (src(0, pl.ds(at, 128)), dst(5, pl.ds(8, 128)), (w_down, n)),
            (src(pl.ds(0, 4), pl.ds(at + 120, 8)), dst(pl.ds(1, 4), pl.ds(0, 8)), (w, n_up)),
            (src(pl.ds(0, 4), pl.ds(at, 8)), dst(pl.ds(1, 4), pl.ds(136, 8)), (w, n_down)),
        )
        copies = []
        for i, (a, b, to) in enumerate(moves):
            copies.append(
                pltpu.make_async_remote_copy(
                    src_ref=a,
                    dst_ref=b,
                    send_sem=sem_hs.at[slot, i],
                    recv_sem=sem_hr.at[slot, i],
                    device_id=to,
                    device_id_type=MESH,
                )
            )
        return copies

    head = halo(0, lambda z, y: temp_ref.at[z, y], 0, lambda z, y: tpad.at[z, y])
    head += halo(1, lambda z, y: phase_ref.at[z, y], 0, lambda z, y: ppad.at[z, y])
    for copy in head:
        copy.start()
    lane = lax.broadcasted_iota(jnp.int32, (8, NX), 1)
    own_k = lax.broadcasted_iota(jnp.int32, (8, NX), 0) % 4 + 4 * me
    ex = jnp.sum(jnp.where(lane == own_k, ex_ref[...], 0.0), axis=1, keepdims=True)
    den = ez_ref[...] + ex[None] + ey_ref[...][None]
    inv_ref[...] = (1.0 / den).reshape(ROWS, NX)
    c_ref[...] = jnp.zeros_like(c_ref)
    d_ref[...] = jnp.zeros_like(d_ref)
    press_ref[...] = jnp.zeros_like(press_ref)
    for load in loads:
        load.wait()

    row8 = lax.broadcasted_iota(jnp.int32, (8, NX), 0)
    lane8 = lax.broadcasted_iota(jnp.int32, (8, NX), 1)

    def around(pad, z, i):
        mid = pl.ds(pl.multiple_of(8 + 8 * i, 8), 8)
        low = pl.ds(pl.multiple_of(8 * i, 8), 8)
        high = pl.ds(pl.multiple_of(16 + 8 * i, 8), 8)
        c = pad[z + 1, mid, :]
        up = pad[z + 1, high, :]
        down = pad[z + 1, low, :]
        near = (
            pad[z + 2, mid, :],
            pad[z, mid, :],
            pltpu.roll(jnp.where(row8 == 0, up, c), 7, 0),
            pltpu.roll(jnp.where(row8 == 7, down, c), 1, 0),
            pltpu.roll(c, NX - 1, 1),
            pltpu.roll(c, 1, 1),
        )
        return c, near

    def sweep(copies, body, carry):
        carry = lax.fori_loop(0, 28, lambda q, c: body(1 + q // 14, 1 + q % 14, c), carry, unroll=4)
        copies[2].wait()
        copies[3].wait()
        carry = lax.fori_loop(0, 4, lambda q, c: body(1 + q // 2, 15 * (q % 2), c), carry)
        copies[0].wait()
        copies[1].wait()
        return lax.fori_loop(0, 32, lambda q, c: body(3 * (q // 16), q % 16, c), carry, unroll=4)

    class Both:
        def __init__(self, a, b):
            self.pair = (a, b)

        def wait(self):
            for copy in self.pair:
                copy.wait()

    def head_chunk(z, i, carry):
        rows = pl.ds(pl.multiple_of(8 * (16 * z + i), 8), 8)
        c, near = around(tpad, z, i)
        pc, pnear = around(ppad, z, i)
        gz = jnp.zeros_like(row8) + (4 * w + z)
        gy = row8 + (n * 128 + 8 * i)
        inside = (gz < NZ - 1, gz > 0, gy < NY - 1, gy > 0, lane8 < NX - 1, lane8 > 0)
        conduct = jnp.where(pc > 0, 1.0, 0.4)
        beta = jnp.where(pc > 0, 1.0, 4.0)
        flux = jnp.zeros_like(c)
        faces = jnp.zeros_like(c)
        for q in range(6):
            ins = jnp.where(inside[q], 1.0, 0.0)
            differ = pnear[q] != pc
            flux = flux + ins * jnp.where(differ, -2.0 * c, near[q] - c)
            faces = faces + ins * jnp.where(differ, 1.0, 0.0)
            wts[q, rows, :] = ins * (0.5 * (beta + jnp.where(pnear[q] > 0, 1.0, 4.0)) - 1.0)
        heated = c + 0.06 * conduct * flux
        tnext_ref[z, pl.ds(pl.multiple_of(8 * i, 8), 8), :] = heated
        mass[rows, :] = 2.0 * conduct * faces * heated
        return carry

    sweep([Both(head[i], head[4 + i]) for i in range(4)], head_chunk, 0)
    stores = [pltpu.make_async_copy(tnext_ref, tnext_any, sem_store.at[8])]
    stores[0].start()
    pl.semaphore_wait(sem_ready, NN - 1)

    ra = lax.broadcasted_iota(jnp.int32, (128, 16), 0)
    ca = lax.broadcasted_iota(jnp.int32, (128, 16), 1)
    pick = jnp.where(ra % 16 == ca, 1.0, 0.0).astype(F32)
    rb = lax.broadcasted_iota(jnp.int32, (128, 128), 0)
    cb = lax.broadcasted_iota(jnp.int32, (128, 128), 1)
    hp = lax.Precision.HIGHEST
    spread = lax.dot_general(pick, north_ref[...], (((1,), (0,)), ((), ())), precision=hp, preferred_element_type=F32)
    spread = lax.dot_general(spread, pick, (((1,), (1,)), ((), ())), precision=hp, preferred_element_type=F32)
    north_all = jnp.where(rb // 16 == cb // 16, spread, 0.0)
    east = east_ref[...]
    for t in range(4):
        lanes = slice(t * 128, (t + 1) * 128)
        across = lax.dot_general(mass[:, lanes], east, (((1,), (1,)), ((), ())), precision=hp, preferred_element_type=F32)
        tile = (rb // 16) * 4 + t
        listed = jnp.zeros((128, 128), F32)
        for e in range(16):
            listed = jnp.where(tile == table_ref[e], 0.3, listed)
        for z in range(4):
            src = lax.dot_general(
                north_all, across[z * 128 : (z + 1) * 128], (((1,), (0,)), ((), ())), precision=hp, preferred_element_type=F32
            )
            f_ref[z * 128 : (z + 1) * 128, lanes] = listed * src
    for z in range(4):
        resid_ref[z] = f_ref[z * 128 : (z + 1) * 128, :]

    half = lax.broadcasted_iota(jnp.int32, (64, 8, 128), 1) < 4
    nn, nt = ((1,), (0,)), ((1,), (1,))

    def parts_of(ref):
        return ref[0], ref[1]

    def bulk(j, src_of, recv, ssem, rsem):
        def send(pw, pn):
            pltpu.make_async_remote_copy(
                src_ref=src_of(pn * NW + pw),
                dst_ref=recv.at[j, me, pl.ds(0, LINES)],
                send_sem=ssem.at[j],
                recv_sem=rsem.at[j],
                device_id=(pw, pn),
                device_id_type=MESH,
            ).start()

        each_peer(w, n, send)

    def wait_others(j, ref, sem):
        part = ref.at[j, pl.ds(0, ND - 1), pl.ds(0, LINES)]
        pltpu.make_async_copy(part, part, sem.at[j]).wait()

    def wait_all(j, ref, sem):
        part = ref.at[j, :, pl.ds(0, LINES)]
        pltpu.make_async_copy(part, part, sem.at[j]).wait()

    def mirrored(piece):
        piece = pltpu.roll(piece, 4, 1)
        return jnp.concatenate([piece[i : i + 1] for i in range(NW - 1, -1, -1)], axis=0)

    def folded(line):
        return line[:, 0:128] + line[:, 128:256] + line[:, 256:384] + line[:, 384:512]

    def summed(rows):
        return jnp.sum(rows, axis=1, keepdims=True)

    def one_pass(j, carry):
        rho, line = carry
        first = j == 0
        table = parts_of(tx_ref)
        low = product(table, split(f_ref[0:256, :]), nt)
        high = product(table, split(f_ref[256:512, :]), nt)
        for zl in range(2):
            a = low[:, zl * 128 : (zl + 1) * 128].reshape(64, 8, 128)
            b = high[:, zl * 128 : (zl + 1) * 128].reshape(64, 8, 128)
            sbf[:, 0, zl * 8 : (zl + 1) * 8, :] = jnp.where(half, a, pltpu.roll(b, 4, 1))
            sbf[:, 1, zl * 8 : (zl + 1) * 8, :] = jnp.where(half, pltpu.roll(a, 4, 1), b)
        sbf[:, :, 16:17, :] = jnp.broadcast_to(line, (64, 2, 1, 128))
        sent = pl.ds(0, LINES)
        own = pltpu.make_async_copy(sbf.at[me // 2, me % 2, sent], recvf.at[j, me, sent], sem_fr.at[j])
        own.start()
        bulk(j, lambda p: sbf.at[p // 2, p % 2, sent], recvf, sem_fs, sem_fr)
        wait_all(j, recvf, sem_fr)
        table = parts_of(ty_ref)
        u = []
        for zl in range(2):
            a = []
            for q in range(NN):
                piece = recvf[j, q * 32 : (q + 1) * 32, zl * 8 : (zl + 1) * 8, :]
                if zl == 1:
                    piece = mirrored(piece)
                a.append(piece.reshape(256, 128))
            u.append(product(split(jnp.concatenate(a, axis=1)), table, nt))
        v = jnp.concatenate(
            [
                product((b_ref[0, 0], b_ref[1, 0]), split(u[0] + u[1]), nn),
                product((b_ref[0, 1], b_ref[1, 1]), split(u[0] - u[1]), nn),
            ],
            axis=0,
        )
        pi = summed(jnp.sum(recvf[j, :, 16:17, :], axis=0))
        alpha = jnp.where(first, -1.0, rho / pi)
        step = jnp.where(first, 0.0, rho / pi)
        left = c_ref[...] - alpha * v
        c_ref[...] = left
        scaled = left * inv_ref[...]
        q_part = jnp.sum(left * scaled, axis=0, keepdims=True)
        sbi[:, 16:17, :] = jnp.broadcast_to(folded(q_part), (ND, 1, 128))
        even = product((bt_ref[0, 0], bt_ref[1, 0]), split(scaled[0:256]), nn)
        odd = product((bt_ref[0, 1], bt_ref[1, 1]), split(scaled[256:512]), nn)
        table = parts_of(ty_ref)
        for zl in range(2):
            r = product(split(even - odd if zl == 1 else even + odd), table, nn)
            for q in range(NN):
                piece = r[:, q * 128 : (q + 1) * 128].reshape(32, 8, 128)
                if zl == 1:
                    piece = mirrored(piece)
                sbi[q * 32 : (q + 1) * 32, zl * 8 : (zl + 1) * 8, :] = piece
        own = pltpu.make_async_copy(sbi.at[me, sent], recvi.at[j, me, sent], sem_ir.at[j])
        own.start()
        bulk(j, lambda p: sbi.at[p, sent], recvi, sem_is, sem_ir)

        def update(g, carry):
            z, i = g // 16, g % 16
            rows = pl.ds(pl.multiple_of(8 * g, 8), 8)
            line = pl.ds(pl.multiple_of(8 * i, 8), 8)
            press_ref[z, line, :] = press_ref[z, line, :] + step * d_ref[rows, :]
            resid_ref[z, line, :] = resid_ref[z, line, :] - step * f_ref[rows, :]
            return carry

        lax.fori_loop(0, 64, update, 0, unroll=4)
        wait_others(j, recvf, sem_fs)
        wait_all(j, recvi, sem_ir)
        wait_others(j, recvi, sem_is)
        def layer(z):
            zl = z % 2
            got = recvi[j, :, zl * 8 : (zl + 1) * 8, :].reshape(64, 2, 8, 128)
            even, odd = got[:, 0], got[:, 1]
            if z < 2:
                rows = jnp.where(half, even, pltpu.roll(odd, 4, 1))
            else:
                rows = jnp.where(half, pltpu.roll(even, 4, 1), odd)
            return rows.reshape(ROWS, 128).T

        table = parts_of(tx_ref)
        field = spad.at[j]
        copies = halo(2 + j, lambda z, y: field.at[(z + 1) if isinstance(z, int) else pl.ds(1, 4), y], 8, lambda z, y: field.at[z, y])
        for z in ((0, 3), (1, 2)):
            r = product(split(jnp.concatenate([layer(q) for q in z], axis=0)), table, nn)
            spad[j, 1 + z[0], 8:136, :] = r[0:128]
            spad[j, 1 + z[1], 8:136, :] = r[128:256]
            if z[0] == 0:
                copies[0].start()
                copies[1].start()
        copies[2].start()
        copies[3].start()
        fresh = summed(jnp.sum(recvi[j, :, 16:17, :], axis=0))
        mix = jnp.where(first, 0.0, fresh / rho)

        def stencil(z, i, carry):
            rows = pl.ds(pl.multiple_of(8 * (16 * z + i), 8), 8)
            c, near = around(field, z, i)
            total = resid_ref[z, pl.ds(pl.multiple_of(8 * i, 8), 8), :] + mix * f_ref[rows, :]
            for q in range(6):
                total = total + wts[q, rows, :] * (c - near[q])
            f_ref[rows, :] = total
            d = c + mix * d_ref[rows, :]
            d_ref[rows, :] = d
            return carry + d * total

        line = jnp.sum(sweep(copies, stencil, jnp.zeros((8, NX), F32)), axis=0, keepdims=True)
        return fresh, folded(line)

    rho, line = lax.fori_loop(0, ITERS, one_pass, (jnp.ones((1, 1), F32), jnp.ones((1, 128), F32)))

    def gather(slots, slot, count, to, ssem, rsem):
        def send(step, carry):
            pltpu.make_async_remote_copy(
                src_ref=slots.at[slot],
                dst_ref=slots.at[slot],
                send_sem=ssem,
                recv_sem=rsem,
                device_id=to(step),
                device_id_type=MESH,
            ).start()
            return carry

        lax.fori_loop(1, count, send, 0)
        part = slots.at[pl.ds(0, count - 1)]
        pltpu.make_async_copy(part, part, rsem).wait()
        pltpu.make_async_copy(part, part, ssem).wait()
        return jnp.sum(slots[...], axis=0)

    y, z, c = w // 8, (w // 2) % 4, w % 2
    mine = n * 2 + c
    red_n[mine] = line
    red_w[w // 2] = gather(
        red_n, mine, 8, lambda t: (w - c + (c + t) % 2, (n + t // 2) % 4), sem_rs.at[0], sem_rr.at[0]
    )
    pi = gather(
        red_w,
        w // 2,
        16,
        lambda t: (((y + t // 4) % 4) * 8 + ((z + t) % 4) * 2 + c, n),
        sem_rs.at[1],
        sem_rr.at[1],
    )
    pi = summed(pi)
    alpha = rho / pi

    for z in range(4):

        def finish(i, carry):
            rows = pl.ds(pl.multiple_of(128 * z + 8 * i, 8), 8)
            line = pl.ds(pl.multiple_of(8 * i, 8), 8)
            press_ref[z, line, :] = press_ref[z, line, :] + alpha * d_ref[rows, :]
            resid_ref[z, line, :] = resid_ref[z, line, :] - alpha * f_ref[rows, :]
            return carry

        lax.fori_loop(0, 16, finish, 0, unroll=4)
        for i, (a, b) in enumerate(((press_ref, press_any), (resid_ref, resid_any))):
            stores.append(pltpu.make_async_copy(a.at[z], b.at[z], sem_store.at[2 * z + i]))
            stores[-1].start()
    for store in stores:
        store.wait()


def hand_on(a, b, c, d, e, f, held, sem_in, sem_out):
    moves = []
    for i, (source, target) in enumerate(((a, d), (b, e), (c, f))):
        for z in (0, 2):
            at = pl.ds(z, 2)
            k = 2 * i + z // 2
            slot = held.at[k]
            moves.append(
                (
                    pltpu.make_async_copy(source.at[at], slot, sem_in.at[k]),
                    pltpu.make_async_copy(slot, target.at[at], sem_out.at[k]),
                )
            )
    for load, _ in moves:
        load.start()
    for load, store in moves:
        load.wait()
        store.start()
    for _, store in moves:
        store.wait()


def on_device(temp, phase, table, north, east):
    ez = np.concatenate([eigen_np(NZ)[0::2], eigen_np(NZ)[1::2]]) + 0.01
    ez = np.repeat(ez, 4).reshape(64, 8, 1).astype(np.float32)
    ey = eigen_np(NY).astype(np.float32).reshape(1, NY)
    ex = eigen_np(NX).astype(np.float32).reshape(1, NX)
    bz = z_table()
    tables = [jnp.asarray(split_np(t)) for t in (cosine_np(NX), cosine_np(NY), bz, bz.transpose(0, 2, 1))]
    vmem = pl.BlockSpec(memory_space=pltpu.VMEM)
    anywhere = pl.BlockSpec(memory_space=pl.ANY)
    tabled = pltpu.VMEM((2, ROWS, ROWS), BF16)
    folded = pltpu.VMEM((2, 2, 256, 256), BF16)
    block = pltpu.VMEM((4, 128, NX), F32)
    smem = pl.BlockSpec(memory_space=pltpu.SMEM)
    shape = jax.ShapeDtypeStruct((4, 128, NX), F32)
    dma = pltpu.SemaphoreType.DMA
    square = pltpu.VMEM((ROWS, NX), F32)
    results = pl.pallas_call(
        whole_kernel,
        out_shape=(shape, shape, shape),
        in_specs=[anywhere, anywhere, smem, vmem, vmem] + [anywhere] * 4 + [vmem] * 3,
        out_specs=(anywhere, anywhere, anywhere),
        scratch_shapes=[
            block,
            block,
            block,
            tabled,
            tabled,
            folded,
            folded,
            pltpu.VMEM((6, 144, NX), F32),
            pltpu.VMEM((6, 144, NX), jnp.int32),
            pltpu.VMEM((ITERS, 6, 144, NX), F32),
            pltpu.VMEM((6, ROWS, NX), F32),
            square,
            square,
            square,
            square,
            square,
            pltpu.VMEM((64, 2, 24, 128), F32),
            pltpu.VMEM((ND, 24, 128), F32),
            pltpu.VMEM((ITERS, ND, 24, 128), F32),
            pltpu.VMEM((ITERS, ND, 24, 128), F32),
            pltpu.VMEM((8, 1, 128), F32),
            pltpu.VMEM((16, 1, 128), F32),
            dma((ITERS,)),
            dma((ITERS,)),
            dma((ITERS,)),
            dma((ITERS,)),
            dma((2,)),
            dma((2,)),
            dma((5, 4)),
            dma((5, 4)),
            pltpu.SemaphoreType.REGULAR,
            dma((6,)),
            dma((9,)),
        ],
        compiler_params=pltpu.CompilerParams(
            collective_id=0, has_side_effects=True, vmem_limit_bytes=60 * 2**20
        ),
    )(temp, phase, table.reshape(16), north, east, *tables, jnp.asarray(ez), jnp.asarray(ey), jnp.asarray(ex))
    return pl.pallas_call(
        hand_on,
        out_shape=(shape, shape, shape),
        in_specs=[anywhere] * 3,
        out_specs=(anywhere, anywhere, anywhere),
        scratch_shapes=[pltpu.VMEM((6, 2, 128, NX), F32), dma((6,)), dma((6,))],
        compiler_params=pltpu.CompilerParams(vmem_limit_bytes=60 * 2**20),
    )(*results)


def solution(mesh):
    block = P("wide", "narrow", None)
    return jax.shard_map(
        on_device,
        mesh=mesh,
        in_specs=(block, block, block, P(), P()),
        out_specs=(block, block, block),
        check_vma=False,
    )
```
